32 devices in a mesh: tile: 8 (over z, y), rank: 4 (over x, core).
Axes of the slice: x: 2, y: 2, z: 4, core: 2. Of those that a mesh axis runs over, the one named last changes fastest.
Arguments:
- step_now: float32 [65536], P(('tile', 'rank')), may hold values from -6 to 6
- residual: float32 [65536], P(('tile', 'rank')), may hold values from -20 to 20
- direction: float32 [65536], P(('tile', 'rank')), may hold values from -20 to 20
- slab_perm: int32 [65536], P(('tile', 'rank')), may hold values from 0 to 2047, as said below
- col_basis: bfloat16 [64, 65536], P(None, ('tile', 'rank')), may hold values from -0.0625 to 0.0625
- row_basis: bfloat16 [64, 6, 32768], P(None, None, ('tile', 'rank')), may hold values from -0.75 to 0.75
- coupling: bfloat16 [8, 8, 64, 64], P('tile'), may hold values from -0.375 to 0.375
- near_blocks: bfloat16 [640, 6, 64, 128], P(('tile', 'rank')), may hold values from -0.5 to 0.5
- near_leaf: int32 [640], P(('tile', 'rank')), may hold values from 0 to 15
- near_target: int32 [640], P(('tile', 'rank')), may hold values from 0 to 191, as said below
- near_live: int32 [32], P(('tile', 'rank')), may hold values from 3 to 20, as said below
- data_weight: float32 [6, 32768], P(None, ('tile', 'rank')), may hold values from 0.25 to 4
Outputs:
- new_step: float32 [65536], P(('tile', 'rank'))
- new_residual: float32 [65536], P(('tile', 'rank'))
- new_direction: float32 [65536], P(('tile', 'rank'))
The draws below stay inside these ranges and needn't reach their ends.
Inputs may be any that keep to these rules, and one draw needn't show every extreme that they name: `slab_perm`: each device's block of 2048 consecutive entries is a permutation of 0 to 2047. The tile offset near_target[g] // 64 is 0, 1 or 2; on every device the first three slots take the offsets 0, 1 and 2 in some order. The first near_live[d] of device d's 20 slots are live.
All inputs are finite; a program needn't handle non-finite values.
Results may differ from the reference program's by a relative error of at most 0.007.
Values may be sent and summed in bfloat16 or wider, within the bound.
A program may use at most 64 MiB of HBM per device.

```python
import math
import jax
import jax.numpy as jnp
from jax import lax

P_DEV = 2048
M_DEV = 1024
R = 64
LEAF = 128
LD = 64
NB = 20
NPRISM = 65536
NDATA = 32768
NBLOCKS = 640
N_TILE = 8
N_RANK = 4


def rising_field(base_scale):
    position = jnp.arange(NPRISM, dtype=jnp.float32) / NPRISM
    return base_scale * 10.0 ** position


def draw_residual(key, part):
    key = jax.random.fold_in(key, 11)
    first, second = jax.random.split(key)
    rough = jnp.exp(jax.random.uniform(second, (NPRISM,), jnp.float32, -0.7, 0.7))
    core = jnp.clip(jax.random.normal(first, (NPRISM,), jnp.float32), -3.0, 3.0)
    return core * rough * rising_field(0.3)


def draw_direction(key, part):
    key = jax.random.fold_in(key, 13)
    first, second = jax.random.split(key)
    rough = jnp.exp(jax.random.uniform(second, (NPRISM,), jnp.float32, -0.7, 0.7))
    core = jnp.clip(jax.random.normal(first, (NPRISM,), jnp.float32), -3.0, 3.0)
    return core * rough * rising_field(0.3)


def draw_slab_perm(key, part):
    key = jax.random.fold_in(key, 5)
    slab_keys = jax.random.split(key, NPRISM // P_DEV)
    orders = jax.vmap(lambda single: jax.random.permutation(single, P_DEV))(slab_keys)
    return orders.reshape(NPRISM).astype(jnp.int32)


def draw_near_target(key, part):
    key = jax.random.fold_in(key, 9)
    first, second, third = jax.random.split(key, 3)
    count = NPRISM // P_DEV
    leaves_tile = M_DEV * N_RANK // LD
    device_keys = jax.random.split(first, count)
    head = jax.vmap(lambda single: jax.random.permutation(single, 3))(device_keys)
    rest = jax.random.randint(second, (count, NB - 3), 0, 3)
    offsets = jnp.concatenate([head.astype(jnp.int32), rest.astype(jnp.int32)], 1)
    data_leaf = jax.random.randint(third, (count, NB), 0, leaves_tile)
    return (offsets * leaves_tile + data_leaf).reshape(NBLOCKS).astype(jnp.int32)


def draw_near_live(key, part):
    key = jax.random.fold_in(key, 7)
    first, second, third = jax.random.split(key, 3)
    count = NPRISM // P_DEV
    draw_one = jax.random.randint(first, (count,), 3, NB + 1)
    draw_two = jax.random.randint(second, (count,), 3, NB + 1)
    counts = jnp.minimum(draw_one, draw_two)
    busiest = jax.random.randint(third, (), 0, count)
    return counts.at[busiest].set(NB).astype(jnp.int32)


def with_ends(drawn, key, least, largest):
    longest = drawn.shape.index(max(drawn.shape))
    spots = []
    for shift in (0, 1):
        where = [jax.random.randint(jax.random.fold_in(key, axis), (), 0, length) for axis, length in enumerate(drawn.shape)]
        where[longest] = (where[longest] + shift) % drawn.shape[longest]
        spots.append(tuple(where))
    return drawn.at[spots[0]].set(least).at[spots[1]].set(largest)


def strengthened(entries, rng, source, target, parts, factor):
    owner, partner = [(jnp.arange(entries.shape[dim]) // (entries.shape[dim] // parts)).reshape([-1 if axis == dim else 1 for axis in range(entries.ndim)]) for dim in (source, target)]
    chosen = jax.random.permutation(rng, parts)[partner]
    strong = (owner == chosen) | (owner == (partner + parts // 2) % parts)
    return jnp.where(strong, factor * entries, entries)


def level_of(stream_key, shape, pieces, low, top_value):
    level = 1.0
    for axis_at, blocks in pieces:
        heights = jax.random.uniform(jax.random.fold_in(jax.random.fold_in(stream_key, 6), axis_at), (blocks,), jnp.float32, low / len(pieces), top_value / len(pieces))
        level = level * jnp.repeat(jnp.exp(heights), shape[axis_at] // blocks).reshape((-1,) + (1,) * (len(shape) - 1 - axis_at))
    return level


def bell_draw(key, extent, scale, most, shards=(), kind=jnp.bfloat16):
    level = level_of(key, extent, shards, -0.22, 0.18) if shards else 1.0
    drawn = jax.random.normal(key, extent, jnp.float32) * scale * level
    return jnp.minimum(jnp.maximum(drawn, -most), most).astype(kind)


def heavy_noise(rng, extent, scale, reach, pieces, heavy, held_as=jnp.bfloat16):
    values = scale * jax.random.normal(rng, extent, jnp.float32)
    if pieces:
        values = values * level_of(rng, extent, pieces, -0.22, 0.18)
    return jnp.clip(strengthened(values, jax.random.fold_in(rng, 3), *heavy), -reach, reach).astype(held_as)


def setup_inputs(seed: int = 0) -> dict:
    arg_keys = jax.random.split(jax.random.key(seed), 13)
    return {
        "step_now": bell_draw(arg_keys[0], (NPRISM,), 1.0, 6.0, ((0, 32),), jnp.float32),
        "residual": draw_residual(jax.random.fold_in(arg_keys[12], 71), 0),
        "direction": draw_direction(jax.random.fold_in(arg_keys[12], 71), 0),
        "slab_perm": draw_slab_perm(jax.random.fold_in(arg_keys[12], 71), 0),
        "col_basis": bell_draw(arg_keys[4], (R, NPRISM), (P_DEV * N_RANK) ** -0.5, 0.0625, ((1, 32),)),
        "row_basis": bell_draw(arg_keys[5], (R, 6, NDATA), R ** -0.5, 0.75, ((2, 32),)),
        "coupling": heavy_noise(arg_keys[6], (N_TILE, N_TILE, R, R), (N_TILE * R) ** -0.5, 0.375, ((0, 8),), (0, 1, 8, 2.0)),
        "near_blocks": bell_draw(arg_keys[7], (NBLOCKS, 6, LD, LEAF), LEAF ** -0.5, 0.5, ((0, 32),)),
        "near_leaf": with_ends(jax.random.randint(arg_keys[8], (NBLOCKS,), 0, P_DEV // LEAF), jax.random.fold_in(arg_keys[8], 1), 0, (P_DEV // LEAF) - 1).astype(jnp.int32),
        "near_target": draw_near_target(jax.random.fold_in(arg_keys[12], 71), 0),
        "near_live": draw_near_live(jax.random.fold_in(arg_keys[12], 71), 0),
        "data_weight": jnp.clip(jnp.exp(math.log(4.0) - 2.7725887 * jax.random.uniform(arg_keys[11], (6, NDATA), jnp.float32) ** level_of(arg_keys[11], (6, NDATA), ((1, 32),), -0.2, 0.2)), 0.25, 4.0),
    }


damping_weight = 0.5
tiny_value = 1e-6


def reference(step_now, residual, direction, slab_perm, col_basis, row_basis, coupling, near_blocks, near_leaf, near_target, near_live, data_weight):
    piece_len = P_DEV // N_TILE
    tile_points = M_DEV * N_RANK
    data_leaves = tile_points // LD
    leaf_count = P_DEV // LEAF
    device_count = N_TILE * N_RANK
    tile_ids = jnp.arange(N_TILE, dtype=jnp.int32)
    far_keep = jnp.abs(tile_ids[:, None] - tile_ids[None, :]) > 1
    dir_bf = direction.astype(jnp.bfloat16).reshape(N_TILE, N_RANK, P_DEV)
    order_map = slab_perm.reshape(N_TILE, N_RANK, P_DEV)
    permuted = jnp.take_along_axis(dir_bf, order_map, axis=2)
    cluster_vec = permuted.reshape(N_TILE, N_RANK, N_TILE, piece_len).transpose(2, 1, 0, 3).reshape(N_TILE, N_RANK * P_DEV)
    basis_f = col_basis.reshape(R, N_TILE, N_RANK * P_DEV).astype(jnp.float32)
    cluster_coef = jnp.einsum("aci,ci->ca", basis_f, cluster_vec.astype(jnp.float32)).astype(jnp.bfloat16)

    def far_row(packed):
        coupled, keep_mask = packed
        masked = cluster_coef * keep_mask[:, None].astype(jnp.bfloat16)
        return jnp.einsum("cab,cb->a", coupled.astype(jnp.float32), masked.astype(jnp.float32))

    far_coef = lax.map(far_row, (coupling, far_keep)).astype(jnp.bfloat16)

    def far_tile(tile_pos):
        basis_tile = lax.dynamic_slice_in_dim(row_basis, tile_pos * tile_points, tile_points, 2).reshape(R, 6 * tile_points)
        return jnp.dot(far_coef[tile_pos], basis_tile, preferred_element_type=jnp.float32)

    far_data = lax.map(far_tile, tile_ids).reshape(N_TILE, 6, tile_points)

    blocks_all = near_blocks.reshape(device_count, NB, 6, LD, LEAF)
    leaves_all = near_leaf.reshape(device_count, NB)
    targets_all = near_target.reshape(device_count, NB)
    vec_all = cluster_vec.reshape(device_count, leaf_count, LEAF)
    slot_ids = jnp.arange(NB, dtype=jnp.int32)

    def near_device(packed):
        near_block, leaf_ids, target_ids, live_count, vector = packed
        live_mask = (slot_ids < live_count).astype(jnp.float32)
        picked = vector[leaf_ids]
        values = jnp.einsum("bkij,bj->bki", near_block.astype(jnp.float32), picked.astype(jnp.float32))
        values = values * live_mask[:, None, None]
        offset = target_ids // data_leaves
        data_leaf = target_ids % data_leaves
        partial_value = jnp.zeros((3, 6, data_leaves, LD), jnp.float32).at[offset, :, data_leaf, :].add(values)
        return partial_value.reshape(3, 6, tile_points)

    partials = lax.map(near_device, (blocks_all, leaves_all, targets_all, near_live, vec_all))
    partials = partials.reshape(N_TILE, N_RANK, 3, 6, tile_points).sum(axis=1)
    zero_rim = jnp.zeros((1, 6, tile_points), jnp.float32)
    near_data = partials[:, 1] + jnp.concatenate([zero_rim, partials[:-1, 2]], 0) + jnp.concatenate([partials[1:, 0], zero_rim], 0)

    weight_tiles = data_weight.reshape(6, N_TILE, tile_points).transpose(1, 0, 2)
    weighted = (weight_tiles * (far_data + near_data)).astype(jnp.bfloat16)

    def back_tile(tile_pos):
        basis_tile = lax.dynamic_slice_in_dim(row_basis, tile_pos * tile_points, tile_points, 2).reshape(R, 6 * tile_points)
        return jnp.dot(basis_tile, weighted[tile_pos].reshape(6 * tile_points), preferred_element_type=jnp.float32)

    back_coef = lax.map(back_tile, tile_ids).astype(jnp.bfloat16)

    def back_row(packed):
        coupled, keep_mask, vector = packed
        spread = jnp.einsum("cab,a->cb", coupled.astype(jnp.float32), vector.astype(jnp.float32))
        return spread * keep_mask[:, None].astype(jnp.float32)

    cluster_back = lax.map(back_row, (coupling, far_keep, back_coef)).sum(axis=0).astype(jnp.bfloat16)
    far_back = jnp.einsum("aci,ca->ci", basis_f, cluster_back.astype(jnp.float32))

    zero_data = jnp.zeros((1, 6, tile_points), jnp.bfloat16)
    padded = jnp.concatenate([zero_data, weighted, zero_data], 0)
    cluster_ids = jnp.arange(device_count, dtype=jnp.int32) // N_RANK

    def near_reverse(packed):
        near_block, leaf_ids, target_ids, live_count, cluster_id = packed
        live_mask = (slot_ids < live_count).astype(jnp.float32)
        window = lax.dynamic_slice_in_dim(padded, cluster_id, 3, 0).reshape(3, 6, data_leaves, LD)
        offset = target_ids // data_leaves
        data_leaf = target_ids % data_leaves
        chosen = window[offset, :, data_leaf, :]
        back_values = jnp.einsum("bkij,bki->bj", near_block.astype(jnp.float32), chosen.astype(jnp.float32))
        back_values = back_values * live_mask[:, None]
        return jnp.zeros((leaf_count, LEAF), jnp.float32).at[leaf_ids].add(back_values).reshape(P_DEV)

    near_back = lax.map(near_reverse, (blocks_all, leaves_all, targets_all, near_live, cluster_ids)).reshape(N_TILE, N_RANK * P_DEV)
    cluster_image = far_back + near_back
    image_perm = cluster_image.reshape(N_TILE, N_RANK, N_TILE, piece_len).transpose(2, 1, 0, 3).reshape(N_TILE, N_RANK, P_DEV)
    inverse = jnp.argsort(order_map, axis=2).astype(jnp.int32)
    slab_image = jnp.take_along_axis(image_perm, inverse, axis=2).reshape(NPRISM)
    normal_image = slab_image + damping_weight * direction
    norm_now = jnp.sum(residual * residual) + tiny_value
    curvature = jnp.sum(direction * normal_image) + tiny_value
    step_size = norm_now / curvature
    new_step = step_now + step_size * direction
    new_residual = residual - step_size * normal_image
    norm_next = jnp.sum(new_residual * new_residual)
    new_direction = new_residual + (norm_next / norm_now) * direction
    return (new_step, new_residual, new_direction)
```

```python
import functools

import jax
import jax.numpy as jnp
from jax import lax
from jax.experimental import pallas as pl
from jax.experimental.pallas import tpu as pltpu
from jax.sharding import PartitionSpec as P

LEAF = 128
LD = 64


damping_weight = 0.5
tiny_value = 1e-06


def with_halo(block, sides, width):
    for axis, dim in sides:
        count = lax.axis_size(axis)
        forward = [(i, i + 1) for i in range(count - 1)]
        backward = [(target, source) for source, target in forward]
        low = lax.ppermute(
            lax.slice_in_dim(block, block.shape[dim] - width, None, axis=dim), axis, forward
        )
        high = lax.ppermute(lax.slice_in_dim(block, 0, width, axis=dim), axis, backward)
        block = jnp.concatenate([low, block, high], axis=dim)
    return block


def per_device(
    step_now,
    residual,
    direction,
    slab_perm,
    col_basis,
    row_basis,
    coupling,
    near_blocks,
    near_leaf,
    near_target,
    near_live,
    data_weight,
):
    tile_count = lax.axis_size("tile")
    rank_count = lax.axis_size("rank")
    tile_here = lax.axis_index("tile")
    slab_len = direction.shape[0]
    piece_len = slab_len // tile_count
    tile_points = data_weight.shape[1] * rank_count
    data_leaves = tile_points // LD
    leaf_count = slab_len // LEAF
    width_rank = col_basis.shape[0]
    block_slots = near_blocks.shape[0]
    dir_bf = direction.astype(jnp.bfloat16)
    outgoing = dir_bf[slab_perm].reshape(tile_count, piece_len)
    cluster_vec = lax.all_to_all(outgoing, "tile", split_axis=0, concat_axis=0, tiled=True).reshape(
        slab_len
    )
    coef_part = jnp.dot(col_basis, cluster_vec, preferred_element_type=jnp.float32)
    coef_all = lax.all_gather(coef_part[None, :], ("tile", "rank"), axis=0, tiled=True)
    cluster_coef = (
        coef_all.reshape(tile_count, rank_count, width_rank).sum(axis=1).astype(jnp.bfloat16)
    )
    far_keep = jnp.abs(jnp.arange(tile_count, dtype=jnp.int32) - tile_here) > 1
    masked_coef = cluster_coef * far_keep[:, None].astype(jnp.bfloat16)
    far_coef = jnp.einsum(
        "cab,cb->a", coupling[0], masked_coef, preferred_element_type=jnp.float32
    ).astype(jnp.bfloat16)
    basis_flat = row_basis.reshape(width_rank, -1)
    far_data = jnp.dot(far_coef, basis_flat, preferred_element_type=jnp.float32).reshape(6, -1)
    live_mask = jnp.arange(block_slots, dtype=jnp.int32) < near_live[0]
    offset = near_target // data_leaves
    data_leaf = near_target % data_leaves
    picked = cluster_vec.reshape(leaf_count, LEAF)[near_leaf]
    values = jnp.einsum("bkij,bj->bki", near_blocks, picked, preferred_element_type=jnp.float32)
    values = values * live_mask[:, None, None].astype(jnp.float32)
    partial_value = (
        jnp.zeros((3, 6, data_leaves, LD), jnp.float32).at[offset, :, data_leaf, :].add(values)
    )
    partial_value = partial_value.reshape(3, 6, tile_points)
    shares = lax.psum_scatter(partial_value, "rank", scatter_dimension=2, tiled=True)
    edges = jnp.stack([shares[0], shares[2]])
    extended = with_halo(edges, (("tile", 0),), 1)
    near_data = shares[1] + extended[0] + extended[3]
    weighted = (data_weight * (far_data + near_data)).astype(jnp.bfloat16)
    back_part = jnp.dot(basis_flat, weighted.reshape(-1), preferred_element_type=jnp.float32)
    back_coef = lax.psum(back_part, "rank").astype(jnp.bfloat16)
    spread = jnp.einsum("cab,a->cb", coupling[0], back_coef, preferred_element_type=jnp.float32)
    spread = spread * far_keep[:, None].astype(jnp.float32)
    cluster_back = lax.psum_scatter(spread, "tile", scatter_dimension=0, tiled=True).astype(
        jnp.bfloat16
    )
    far_back = jnp.dot(cluster_back[0], col_basis, preferred_element_type=jnp.float32)
    tile_data = lax.all_gather(weighted, "rank", axis=1, tiled=True)
    window = with_halo(tile_data[None], (("tile", 0),), 1)
    chosen = window.reshape(3, 6, data_leaves, LD)[offset, :, data_leaf, :]
    back_values = jnp.einsum(
        "bkij,bki->bj", near_blocks, chosen, preferred_element_type=jnp.float32
    )
    back_values = back_values * live_mask[:, None].astype(jnp.float32)
    near_back = (
        jnp.zeros((leaf_count, LEAF), jnp.float32).at[near_leaf].add(back_values).reshape(slab_len)
    )
    cluster_image = far_back + near_back
    returned = lax.all_to_all(
        cluster_image.reshape(tile_count, piece_len),
        "tile",
        split_axis=0,
        concat_axis=0,
        tiled=True,
    ).reshape(slab_len)
    slab_image = jnp.zeros((slab_len,), jnp.float32).at[slab_perm].set(returned)
    normal_image = slab_image + damping_weight * direction
    norm_now, curvature = lax.psum(
        (jnp.sum(residual * residual), jnp.sum(direction * normal_image)), ("tile", "rank")
    )
    norm_now = norm_now + tiny_value
    step_size = norm_now / (curvature + tiny_value)
    new_step = step_now + step_size * direction
    new_residual = residual - step_size * normal_image
    norm_next = lax.psum(jnp.sum(new_residual * new_residual), ("tile", "rank"))
    new_direction = new_residual + norm_next / norm_now * direction
    return (new_step, new_residual, new_direction)


def split_bf16(x, parts):
    out = []
    for _ in range(parts):
        head = x.astype(jnp.bfloat16)
        out.append(head)
        x = x - head.astype(jnp.float32)
    return out


def dot_nt(a, b):
    return lax.dot_general(a, b, (((1,), (1,)), ((), ())), preferred_element_type=jnp.float32)


def dot_nn(a, b):
    return jnp.dot(a, b, preferred_element_type=jnp.float32)


def iota(shape, dim):
    return lax.broadcasted_iota(jnp.int32, shape, dim)


def cg_kernel(
    dims,
    residual_ref,
    direction_ref,
    perm_ref,
    col_hbm,
    row_hbm,
    coupling_hbm,
    blocks_hbm,
    leaf_ref,
    target_ref,
    live_ref,
    weight_ref,
    image_out,
    alpha_out,
    beta_out,
    col_ref,
    row_ref,
    coupling_ref,
    blocks_ref,
    onehot_ref,
    slots_ref,
    weight_s,
    far_s,
    weighted_f,
    a_send,
    a_recv,
    vec_f,
    res_f,
    b_send,
    b_recv,
    c_send,
    c_recv,
    d_send,
    d_recv,
    e_send,
    e_recv,
    far_back_s,
    image_s,
    f_recv,
    g_send,
    g_recv,
    values_s,
    load_sem,
    a_ss,
    a_rs,
    b_ss,
    b_rs,
    c_ss,
    c_rs,
    d_ss,
    d_rs,
    e_ss,
    e_rs,
    f_ss,
    f_rs,
    g_ss,
    g_rs,
):
    T, RK, NBS, KC, WR = dims
    bf16, f32 = jnp.bfloat16, jnp.float32
    rows = direction_ref.shape[0]
    pr = rows // T
    G = weight_ref.shape[1] // 128
    KG = KC * G
    gt = G * RK
    NBP = values_s.shape[0]
    KI = KC * LD
    t = lax.axis_index("tile")
    r = lax.axis_index("rank")
    me = t * RK + r

    def remote(src, dst, ss, rs, tile, rank):
        return pltpu.make_async_remote_copy(
            src_ref=src,
            dst_ref=dst,
            send_sem=ss,
            recv_sem=rs,
            device_id=(tile, rank),
            device_id_type=pl.DeviceIdType.MESH,
        )

    loads = [
        pltpu.make_async_copy(col_hbm, col_ref, load_sem.at[0]),
        pltpu.make_async_copy(blocks_hbm, blocks_ref, load_sem.at[1]),
        pltpu.make_async_copy(coupling_hbm, coupling_ref, load_sem.at[2]),
        pltpu.make_async_copy(row_hbm, row_ref, load_sem.at[3]),
    ]
    for load in loads:
        load.start()

    b_recv[...] = jnp.zeros_like(b_recv)
    e_recv[...] = jnp.zeros_like(e_recv)
    c_recv[...] = jnp.zeros_like(c_recv)
    d_recv[...] = jnp.zeros_like(d_recv)

    barrier = pltpu.get_barrier_semaphore()
    for dt in range(T):
        for dr in range(RK):
            if dt or dr:
                pl.semaphore_signal(
                    barrier,
                    inc=1,
                    device_id=(lax.rem(t + dt, T), lax.rem(r + dr, RK)),
                    device_id_type=pl.DeviceIdType.MESH,
                )

    pieces = jnp.concatenate(
        split_bf16(direction_ref[...], 3) + split_bf16(residual_ref[...], 3), axis=0
    )
    for q in range(rows):
        perm = perm_ref[q : q + 1, :]
        low = lax.bitwise_and(perm, 127)
        high = lax.shift_right_logical(perm, 7)
        onehot = (iota((128, 128), 0) == low).astype(f32).astype(bf16)
        onehot_ref[q] = onehot
        looked = dot_nn(pieces, onehot)
        mask = iota((rows, 128), 0) == high
        d_rows = (looked[0:rows] + looked[rows : 2 * rows]) + looked[2 * rows : 3 * rows]
        r_rows = (looked[3 * rows : 4 * rows] + looked[4 * rows : 5 * rows]) + looked[5 * rows :]
        c, k = q // pr, q % pr
        a_send[c, k : k + 1, :] = jnp.sum(jnp.where(mask, d_rows, 0.0), axis=0, keepdims=True)
        a_send[c, pr + k : pr + k + 1, :] = jnp.sum(
            jnp.where(mask, r_rows, 0.0), axis=0, keepdims=True
        )

    pl.semaphore_wait(barrier, T * RK - 1)

    a_recv[t] = a_send[t]
    for off in range(1, T):
        c = lax.rem(t + off, T)
        remote(a_send.at[c], a_recv.at[t], a_ss.at[c], a_rs.at[t], c, r).start()

    slots_ref[...] = jnp.zeros_like(slots_ref)
    slots_ref[0:1, 0:NBS] = target_ref[...]
    slots_ref[1:2, 0:NBS] = leaf_ref[...]
    diagonal = iota((NBP, 128), 0) == iota((NBP, 128), 1)
    target_row = slots_ref[0:1, :]
    leaf_row = slots_ref[1:2, :]
    target_col = jnp.sum(jnp.where(diagonal, target_row, 0), axis=1, keepdims=True)
    leaf_col = jnp.sum(jnp.where(diagonal, leaf_row, 0), axis=1, keepdims=True)
    live = iota((1, 128), 1) < live_ref[...]
    spread_hot = (
        ((iota((3 * gt, 128), 0) == lax.shift_right_logical(target_row, 1)) & live)
        .astype(f32)
        .astype(bf16)[:, :NBP]
    )
    pick_hot = (iota((NBP, 3 * gt), 1) == lax.shift_right_logical(target_col, 1)).astype(f32).astype(bf16)
    leaf_hot = (iota((NBP, rows), 1) == leaf_col).astype(f32).astype(bf16)
    leaf_spread = ((iota((rows, 128), 0) == leaf_row) & live).astype(f32).astype(bf16)[:, :NBP]
    odd = lax.bitwise_and(target_col, 1) == 1
    upper = iota((NBP, 128), 1) >= LD
    for k in range(KC):
        for g in range(G):
            weight_s[k * G + g : k * G + g + 1, :] = weight_ref[k : k + 1, g * 128 : (g + 1) * 128]
    values_s[...] = jnp.zeros_like(values_s)
    loads[0].wait()
    loads[1].wait()

    for off in range(1, T):
        s = lax.rem(t + off, T)
        remote(a_send.at[s], a_recv.at[s], a_ss.at[s], a_rs.at[s], s, r).wait_recv()
    for s in range(T):
        vec_f[s * pr : (s + 1) * pr, :] = a_recv[s, 0:pr, :]
        res_f[s * pr : (s + 1) * pr, :] = a_recv[s, pr : 2 * pr, :]

    vec_row = jnp.concatenate([vec_f[q : q + 1, :] for q in range(rows)], axis=1).astype(bf16)
    b_send[:, 0:WR] = dot_nt(vec_row, col_ref[...])

    def far(c):
        return jnp.abs(c - t) > 1

    for off in range(1, T):
        c = lax.rem(t + off, T)

        @pl.when(far(c))
        def _():
            for k in range(RK):
                remote(
                    b_send, b_recv.at[me], b_ss.at[c * RK + k], b_rs.at[me], c, k
                ).start()

    picked = dot_nn(leaf_hot, vec_f[...].astype(bf16)).astype(bf16)
    for b in range(NBS):
        values_s[b : b + 1, :] = dot_nt(
            picked[b : b + 1, :], blocks_ref[b * KI : (b + 1) * KI, :]
        )
    for k in range(KC):
        part = values_s[:, (k // 2) * 128 : (k // 2 + 1) * 128]
        rolled = pltpu.roll(part, LD, 1)
        moved = jnp.where(odd, rolled, part) if k % 2 == 0 else jnp.where(odd, part, rolled)
        moved = jnp.where(upper == odd, moved, 0.0)
        head, tail = split_bf16(moved, 2)
        summed = dot_nn(spread_hot, head) + dot_nn(spread_hot, tail)
        for o in range(3):
            for k2 in range(RK):
                start = o * gt + k2 * G
                c_send[o, k2, k * G : (k + 1) * G, :] = summed[start : start + G, :]
    for o in range(3):
        for k2 in range(RK):
            c_out = c_send[o, k2].astype(bf16)
            c_bf = c_out
            d_send[1 + o * RK + k2] = c_bf

    def inside(c):
        return (c >= 0) & (c < T)

    def near_copies(source, landing, ss, rs, mirrored, act):
        for o in (0, 2, 1):
            there = t + (1 - o if mirrored else o - 1)

            @pl.when(inside(there))
            def _():
                for dr in range(RK):
                    if o == 1 and dr == 0:
                        continue
                    k2 = lax.rem(r + dr, RK)
                    act(
                        remote(
                            source(o, k2), landing.at[o, r], ss.at[o, k2], rs.at[o, r], there, k2
                        )
                    )

    def near_waits(landing, ss, rs, mirrored):
        for o in (1, 0, 2):
            there = t + (o - 1 if mirrored else 1 - o)

            @pl.when(inside(there))
            def _():
                for dr in range(RK):
                    if o == 1 and dr == 0:
                        continue
                    k2 = lax.rem(r + dr, RK)
                    remote(
                        landing.at[o, k2], landing.at[o, k2], ss.at[o, k2], rs.at[o, k2], t, k2
                    ).wait_recv()

    def c_source(o, k2):
        return d_send.at[1 + o * RK + k2]

    def d_source(o, k2):
        return d_send.at[0]

    near_copies(c_source, c_recv, c_ss, c_rs, False, lambda copy: copy.start())

    loads[2].wait()
    loads[3].wait()
    for off in range(1, T):
        c = lax.rem(t + off, T)

        @pl.when(far(c))
        def _():
            for k in range(RK):
                slot = c * RK + k
                remote(b_send, b_recv.at[slot], b_ss.at[slot], b_rs.at[slot], c, k).wait_recv()

    far_coef = jnp.zeros((1, WR), f32)
    for c in range(T):
        coef = b_recv[c * RK]
        for k in range(1, RK):
            coef = coef + b_recv[c * RK + k]
        far_coef = far_coef + dot_nt(coef[:, 0:WR].astype(bf16), coupling_ref[c])
    far_row = dot_nn(far_coef.astype(bf16), row_ref[...])
    for m in range(KG):
        far_s[m : m + 1, :] = far_row[:, m * 128 : (m + 1) * 128]

    near_waits(c_recv, c_ss, c_rs, False)
    own = jnp.zeros((KG, 128), f32)
    for k2 in range(RK):
        own = own + jnp.where(r == k2, c_send[1, k2], 0.0)
    near = own
    for o in range(3):
        for k2 in range(RK):
            near = near + c_recv[o, k2].astype(f32)
    weighted = (weight_s[...] * (far_s[...] + near)).astype(bf16)
    d_send[0] = weighted
    weighted_f[...] = weighted.astype(f32)
    near_copies(d_source, d_recv, d_ss, d_rs, True, lambda copy: copy.start())
    d_recv[1, r] = weighted

    weighted_row = jnp.concatenate([weighted_f[m : m + 1, :] for m in range(KG)], axis=1)
    back_part = dot_nt(weighted_row.astype(bf16), row_ref[...])
    back_two = jnp.concatenate(split_bf16(back_part, 2), axis=0)
    for c in range(T):
        two = dot_nn(back_two, coupling_ref[c])
        e_send[c, :, 0:WR] = two[0:1, :] + two[1:2, :]
    for off in range(1, T):
        c = lax.rem(t + off, T)

        @pl.when(far(c))
        def _():
            for k in range(RK):
                remote(
                    e_send.at[c], e_recv.at[me], e_ss.at[c * RK + k], e_rs.at[me], c, k
                ).start()

    near_waits(d_recv, d_ss, d_rs, True)
    chosen = []
    for k in range(KC):
        window = jnp.concatenate(
            [
                d_recv[o, k2, :, :].astype(f32)[k * G : (k + 1) * G, :]
                for o in range(3)
                for k2 in range(RK)
            ],
            axis=0,
        ).astype(bf16)
        found = dot_nn(pick_hot, window)
        rolled = pltpu.roll(found, LD, 1)
        chosen.append(
            jnp.where(odd, rolled, found) if k % 2 == 0 else jnp.where(odd, found, rolled)
        )
    chosen_rows = jnp.concatenate(
        [jnp.where(upper, chosen[2 * m + 1], chosen[2 * m]) for m in range(KC // 2)], axis=1
    ).astype(bf16)
    for b in range(NBS):
        values_s[b : b + 1, 0:128] = dot_nn(
            chosen_rows[b : b + 1, :], blocks_ref[b * KI : (b + 1) * KI, :]
        )
    head, tail = split_bf16(values_s[:, 0:128], 2)
    near_back = dot_nn(leaf_spread, head) + dot_nn(leaf_spread, tail)

    for off in range(1, T):
        c = lax.rem(t + off, T)

        @pl.when(far(c))
        def _():
            for k in range(RK):
                slot = c * RK + k
                remote(e_send.at[c], e_recv.at[slot], e_ss.at[slot], e_rs.at[slot], c, k).wait_recv()

    cluster_back = jnp.zeros((1, 128), f32)
    for slot in range(T * RK):
        cluster_back = cluster_back + e_recv[slot]
    far_back = dot_nn(cluster_back[:, 0:WR].astype(bf16), col_ref[...])
    for q in range(rows):
        far_back_s[q : q + 1, :] = far_back[:, q * 128 : (q + 1) * 128]
    image = far_back_s[...] + near_back
    for s in range(T):
        image_s[s] = image[s * pr : (s + 1) * pr, :]
    for off in range(1, T):
        s = lax.rem(t + off, T)
        remote(image_s.at[s], f_recv.at[t], f_ss.at[s], f_rs.at[t], s, r).start()
    f_recv[t] = image_s[t]

    vec = vec_f[...]
    res = res_f[...]
    normal = image + damping_weight * vec

    def total(x):
        return jnp.sum(jnp.sum(x, axis=0, keepdims=True), axis=1, keepdims=True)

    lane = iota((1, 128), 1)
    sums = jnp.where(lane == 0, total(vec * normal), 0.0)
    sums = jnp.where(lane == 1, total(res * normal), sums)
    sums = jnp.where(lane == 2, total(normal * normal), sums)
    sums = jnp.where(lane == 3, total(res * res), sums)
    g_send[...] = sums
    g_recv[me] = sums
    others = [(dt, dr) for dt in range(T) for dr in range(RK) if dt or dr]
    for dt, dr in others:
        c, k = lax.rem(t + dt, T), lax.rem(r + dr, RK)
        remote(g_send, g_recv.at[me], g_ss.at[c * RK + k], g_rs.at[me], c, k).start()

    for off in range(1, T):
        s = lax.rem(t + off, T)
        remote(image_s.at[s], f_recv.at[s], f_ss.at[s], f_rs.at[s], s, r).wait_recv()
    back = jnp.zeros((3 * rows, 128), f32)
    for q in range(rows):
        perm = perm_ref[q : q + 1, :]
        high = lax.shift_right_logical(perm, 7)
        mask = iota((rows, 128), 0) == high
        entry = f_recv[q // pr, q % pr : q % pr + 1, :]
        parts = split_bf16(jnp.where(mask, entry, 0.0), 3)
        back = back + dot_nt(jnp.concatenate(parts, axis=0), onehot_ref[q])
    slab = (back[0:rows] + back[rows : 2 * rows]) + back[2 * rows :]
    image_out[...] = slab + damping_weight * direction_ref[...]

    for dt, dr in others:
        c, k = lax.rem(t + dt, T), lax.rem(r + dr, RK)
        slot = c * RK + k
        remote(g_send, g_recv.at[slot], g_ss.at[slot], g_rs.at[slot], c, k).wait_recv()
    sums = g_recv[0]
    for slot in range(1, T * RK):
        sums = sums + g_recv[slot]

    def pick(i):
        return jnp.sum(jnp.where(lane == i, sums, 0.0), axis=1, keepdims=True)

    norm_now = pick(3) + tiny_value
    alpha = norm_now / (pick(0) + tiny_value)
    norm_next = pick(3) - 2.0 * alpha * pick(1) + alpha * alpha * pick(2)
    beta = jnp.maximum(norm_next, 0.0) / norm_now
    alpha_out[...] = jnp.broadcast_to(alpha, alpha_out.shape)
    beta_out[...] = jnp.broadcast_to(beta, beta_out.shape)

    for off in range(1, T):
        c = lax.rem(t + off, T)
        remote(a_send.at[c], a_recv.at[t], a_ss.at[c], a_rs.at[t], c, r).wait_send()
        remote(image_s.at[c], f_recv.at[t], f_ss.at[c], f_rs.at[t], c, r).wait_send()

        @pl.when(far(c))
        def _():
            for k in range(RK):
                remote(b_send, b_recv.at[me], b_ss.at[c * RK + k], b_rs.at[me], c, k).wait_send()
                remote(
                    e_send.at[c], e_recv.at[me], e_ss.at[c * RK + k], e_rs.at[me], c, k
                ).wait_send()

    near_copies(c_source, c_recv, c_ss, c_rs, False, lambda copy: copy.wait_send())
    near_copies(d_source, d_recv, d_ss, d_rs, True, lambda copy: copy.wait_send())
    for dt, dr in others:
        c, k = lax.rem(t + dt, T), lax.rem(r + dr, RK)
        remote(g_send, g_recv.at[me], g_ss.at[c * RK + k], g_rs.at[me], c, k).wait_send()


def fused(
    step_now,
    residual,
    direction,
    slab_perm,
    col_basis,
    row_basis,
    coupling,
    near_blocks,
    near_leaf,
    near_target,
    near_live,
    data_weight,
):
    T, RK = lax.axis_size("tile"), lax.axis_size("rank")
    N = T * RK
    rows = direction.shape[0] // 128
    pr = rows // T
    NBS, KC = near_blocks.shape[0], near_blocks.shape[1]
    WR = col_basis.shape[0]
    G = data_weight.shape[1] // 128
    KG = KC * G
    NBP = -(-NBS // 16) * 16
    f32, bf16 = jnp.float32, jnp.bfloat16
    res2 = residual.reshape(rows, 128)
    dir2 = direction.reshape(rows, 128)
    vmem = pl.BlockSpec(memory_space=pltpu.VMEM)
    hbm = pl.BlockSpec(memory_space=pl.ANY)
    row2 = row_basis.reshape(WR, -1)
    blocks2 = near_blocks.reshape(-1, LEAF)
    sem = pltpu.SemaphoreType.DMA
    out = jax.ShapeDtypeStruct((rows, 128), f32)
    image, alpha, beta = pl.pallas_call(
        functools.partial(cg_kernel, (T, RK, NBS, KC, WR)),
        out_shape=(out, out, out),
        in_specs=[vmem, vmem, vmem, hbm, hbm, hbm, hbm, vmem, vmem, vmem, vmem],
        out_specs=(vmem, vmem, vmem),
        scratch_shapes=[
            pltpu.VMEM(col_basis.shape, bf16),
            pltpu.VMEM(row2.shape, bf16),
            pltpu.VMEM(coupling.shape[1:], bf16),
            pltpu.VMEM(blocks2.shape, bf16),
            pltpu.VMEM((rows, 128, 128), bf16),
            pltpu.VMEM((8, 128), jnp.int32),
            pltpu.VMEM((KG, 128), f32),
            pltpu.VMEM((KG, 128), f32),
            pltpu.VMEM((KG, 128), f32),
            pltpu.VMEM((T, 2 * pr, 128), f32),
            pltpu.VMEM((T, 2 * pr, 128), f32),
            pltpu.VMEM((rows, 128), f32),
            pltpu.VMEM((rows, 128), f32),
            pltpu.VMEM((1, 128), f32),
            pltpu.VMEM((N, 1, 128), f32),
            pltpu.VMEM((3, RK, KG, 128), f32),
            pltpu.VMEM((3, RK, KG, 128), bf16),
            pltpu.VMEM((1 + 3 * RK, KG, 128), bf16),
            pltpu.VMEM((3, RK, KG, 128), bf16),
            pltpu.VMEM((T, 1, 128), f32),
            pltpu.VMEM((N, 1, 128), f32),
            pltpu.VMEM((rows, 128), f32),
            pltpu.VMEM((T, pr, 128), f32),
            pltpu.VMEM((T, pr, 128), f32),
            pltpu.VMEM((1, 128), f32),
            pltpu.VMEM((N, 1, 128), f32),
            pltpu.VMEM((NBP, KC * LD), f32),
            sem((4,)),
            sem((T,)),
            sem((T,)),
            sem((N,)),
            sem((N,)),
            sem((3, RK)),
            sem((3, RK)),
            sem((3, RK)),
            sem((3, RK)),
            sem((N,)),
            sem((N,)),
            sem((T,)),
            sem((T,)),
            sem((N,)),
            sem((N,)),
        ],
        compiler_params=pltpu.CompilerParams(
            collective_id=0, has_side_effects=True, vmem_limit_bytes=32 * 1024 * 1024
        ),
    )(
        res2,
        dir2,
        slab_perm.reshape(rows, 128),
        col_basis,
        row2,
        coupling[0],
        blocks2,
        near_leaf.reshape(1, NBS),
        near_target.reshape(1, NBS),
        near_live.reshape(1, 1),
        data_weight,
    )
    new_step = step_now.reshape(rows, 128) + alpha * dir2
    new_residual = res2 - alpha * image
    new_direction = new_residual + beta * dir2
    return tuple(x.reshape(-1) for x in (new_step, new_residual, new_direction))


def solution(mesh):
    def body(*args):
        piece = args[2].shape[0] // mesh.shape["tile"]
        return (per_device if piece % 128 else fused)(*args)

    return jax.shard_map(
        body,
        mesh=mesh,
        in_specs=(
            P(("tile", "rank")),
            P(("tile", "rank")),
            P(("tile", "rank")),
            P(("tile", "rank")),
            P(None, ("tile", "rank")),
            P(None, None, ("tile", "rank")),
            P("tile", None, None, None),
            P(("tile", "rank"), None, None, None),
            P(("tile", "rank")),
            P(("tile", "rank")),
            P(("tile", "rank")),
            P(None, ("tile", "rank")),
        ),
        out_specs=(P(("tile", "rank")), P(("tile", "rank")), P(("tile", "rank"))),
        check_vma=False,
    )
```

```python
import functools

import jax
import jax.numpy as jnp
from jax import lax
from jax.experimental import pallas as pl
from jax.experimental.pallas import tpu as pltpu
from jax.sharding import PartitionSpec as P

LEAF = 128
LD = 64


damping_weight = 0.5
tiny_value = 1e-06


def with_halo(block, sides, width):
    for axis, dim in sides:
        count = lax.axis_size(axis)
        forward = [(i, i + 1) for i in range(count - 1)]
        backward = [(target, source) for source, target in forward]
        low = lax.ppermute(
            lax.slice_in_dim(block, block.shape[dim] - width, None, axis=dim), axis, forward
        )
        high = lax.ppermute(lax.slice_in_dim(block, 0, width, axis=dim), axis, backward)
        block = jnp.concatenate([low, block, high], axis=dim)
    return block


def per_device(
    step_now,
    residual,
    direction,
    slab_perm,
    col_basis,
    row_basis,
    coupling,
    near_blocks,
    near_leaf,
    near_target,
    near_live,
    data_weight,
):
    tile_count = lax.axis_size("tile")
    rank_count = lax.axis_size("rank")
    tile_here = lax.axis_index("tile")
    slab_len = direction.shape[0]
    piece_len = slab_len // tile_count
    tile_points = data_weight.shape[1] * rank_count
    data_leaves = tile_points // LD
    leaf_count = slab_len // LEAF
    width_rank = col_basis.shape[0]
    block_slots = near_blocks.shape[0]
    dir_bf = direction.astype(jnp.bfloat16)
    outgoing = dir_bf[slab_perm].reshape(tile_count, piece_len)
    cluster_vec = lax.all_to_all(outgoing, "tile", split_axis=0, concat_axis=0, tiled=True).reshape(
        slab_len
    )
    coef_part = jnp.dot(col_basis, cluster_vec, preferred_element_type=jnp.float32)
    coef_all = lax.all_gather(coef_part[None, :], ("tile", "rank"), axis=0, tiled=True)
    cluster_coef = (
        coef_all.reshape(tile_count, rank_count, width_rank).sum(axis=1).astype(jnp.bfloat16)
    )
    far_keep = jnp.abs(jnp.arange(tile_count, dtype=jnp.int32) - tile_here) > 1
    masked_coef = cluster_coef * far_keep[:, None].astype(jnp.bfloat16)
    far_coef = jnp.einsum(
        "cab,cb->a", coupling[0], masked_coef, preferred_element_type=jnp.float32
    ).astype(jnp.bfloat16)
    basis_flat = row_basis.reshape(width_rank, -1)
    far_data = jnp.dot(far_coef, basis_flat, preferred_element_type=jnp.float32).reshape(6, -1)
    live_mask = jnp.arange(block_slots, dtype=jnp.int32) < near_live[0]
    offset = near_target // data_leaves
    data_leaf = near_target % data_leaves
    picked = cluster_vec.reshape(leaf_count, LEAF)[near_leaf]
    values = jnp.einsum("bkij,bj->bki", near_blocks, picked, preferred_element_type=jnp.float32)
    values = values * live_mask[:, None, None].astype(jnp.float32)
    partial_value = (
        jnp.zeros((3, 6, data_leaves, LD), jnp.float32).at[offset, :, data_leaf, :].add(values)
    )
    partial_value = partial_value.reshape(3, 6, tile_points)
    shares = lax.psum_scatter(partial_value, "rank", scatter_dimension=2, tiled=True)
    edges = jnp.stack([shares[0], shares[2]])
    extended = with_halo(edges, (("tile", 0),), 1)
    near_data = shares[1] + extended[0] + extended[3]
    weighted = (data_weight * (far_data + near_data)).astype(jnp.bfloat16)
    back_part = jnp.dot(basis_flat, weighted.reshape(-1), preferred_element_type=jnp.float32)
    back_coef = lax.psum(back_part, "rank").astype(jnp.bfloat16)
    spread = jnp.einsum("cab,a->cb", coupling[0], back_coef, preferred_element_type=jnp.float32)
    spread = spread * far_keep[:, None].astype(jnp.float32)
    cluster_back = lax.psum_scatter(spread, "tile", scatter_dimension=0, tiled=True).astype(
        jnp.bfloat16
    )
    far_back = jnp.dot(cluster_back[0], col_basis, preferred_element_type=jnp.float32)
    tile_data = lax.all_gather(weighted, "rank", axis=1, tiled=True)
    window = with_halo(tile_data[None], (("tile", 0),), 1)
    chosen = window.reshape(3, 6, data_leaves, LD)[offset, :, data_leaf, :]
    back_values = jnp.einsum(
        "bkij,bki->bj", near_blocks, chosen, preferred_element_type=jnp.float32
    )
    back_values = back_values * live_mask[:, None].astype(jnp.float32)
    near_back = (
        jnp.zeros((leaf_count, LEAF), jnp.float32).at[near_leaf].add(back_values).reshape(slab_len)
    )
    cluster_image = far_back + near_back
    returned = lax.all_to_all(
        cluster_image.reshape(tile_count, piece_len),
        "tile",
        split_axis=0,
        concat_axis=0,
        tiled=True,
    ).reshape(slab_len)
    slab_image = jnp.zeros((slab_len,), jnp.float32).at[slab_perm].set(returned)
    normal_image = slab_image + damping_weight * direction
    norm_now, curvature = lax.psum(
        (jnp.sum(residual * residual), jnp.sum(direction * normal_image)), ("tile", "rank")
    )
    norm_now = norm_now + tiny_value
    step_size = norm_now / (curvature + tiny_value)
    new_step = step_now + step_size * direction
    new_residual = residual - step_size * normal_image
    norm_next = lax.psum(jnp.sum(new_residual * new_residual), ("tile", "rank"))
    new_direction = new_residual + norm_next / norm_now * direction
    return (new_step, new_residual, new_direction)


def split_bf16(x, parts):
    out = []
    for _ in range(parts):
        head = x.astype(jnp.bfloat16)
        out.append(head)
        x = x - head.astype(jnp.float32)
    return out


def dot_nt(a, b):
    return lax.dot_general(a, b, (((1,), (1,)), ((), ())), preferred_element_type=jnp.float32)


def dot_nn(a, b):
    return jnp.dot(a, b, preferred_element_type=jnp.float32)


def iota(shape, dim):
    return lax.broadcasted_iota(jnp.int32, shape, dim)


def cg_kernel(
    dims,
    residual_hbm,
    direction_hbm,
    perm_hbm,
    col_hbm,
    row_hbm,
    coupling_hbm,
    blocks_hbm,
    leaf_hbm,
    target_hbm,
    live_smem,
    weight_hbm,
    image_out,
    alpha_out,
    beta_out,
    residual_ref,
    direction_ref,
    perm_ref,
    leaf_ref,
    target_ref,
    weight_ref,
    col_ref,
    row_ref,
    coupling_ref,
    blocks_ref,
    onehot_ref,
    slots_ref,
    weight_s,
    far_s,
    weighted_f,
    a_send,
    a_recv,
    vec_f,
    res_f,
    b_send,
    b_recv,
    c_send,
    c_recv,
    d_send,
    d_recv,
    e_send,
    e_recv,
    far_back_s,
    image_s,
    f_recv,
    g_send,
    g_recv,
    values_s,
    load_sem,
    a_ss,
    a_rs,
    b_ss,
    b_rs,
    c_ss,
    c_rs,
    d_ss,
    d_rs,
    e_ss,
    e_rs,
    f_ss,
    f_rs,
    g_ss,
    g_rs,
):
    T, RK, NBS, KC, WR = dims
    bf16, f32 = jnp.bfloat16, jnp.float32
    rows = direction_hbm.shape[0]
    pr = rows // T
    G = weight_hbm.shape[1] // 128
    KG = KC * G
    gt = G * RK
    NBP = values_s.shape[0]
    KI = KC * LD
    t = lax.axis_index("tile")
    r = lax.axis_index("rank")
    me = t * RK + r

    def remote(src, dst, ss, rs, tile, rank):
        return pltpu.make_async_remote_copy(
            src_ref=src,
            dst_ref=dst,
            send_sem=ss,
            recv_sem=rs,
            device_id=(tile, rank),
            device_id_type=pl.DeviceIdType.MESH,
        )

    operands = [
        (direction_hbm, direction_ref),
        (perm_hbm, perm_ref),
        (residual_hbm, residual_ref),
        (leaf_hbm, leaf_ref),
        (target_hbm, target_ref),
        (weight_hbm, weight_ref),
        (col_hbm, col_ref),
        (blocks_hbm, blocks_ref),
        (coupling_hbm, coupling_ref),
        (row_hbm, row_ref),
    ]
    loads = [
        pltpu.make_async_copy(source, held, load_sem.at[i])
        for i, (source, held) in enumerate(operands)
    ]
    for load in loads:
        load.start()

    b_recv[...] = jnp.zeros_like(b_recv)
    e_recv[...] = jnp.zeros_like(e_recv)
    c_recv[...] = jnp.zeros_like(c_recv)
    d_recv[...] = jnp.zeros_like(d_recv)

    barrier = pltpu.get_barrier_semaphore()
    for dt in range(T):
        for dr in range(RK):
            if dt or dr:
                pl.semaphore_signal(
                    barrier,
                    inc=1,
                    device_id=(lax.rem(t + dt, T), lax.rem(r + dr, RK)),
                    device_id_type=pl.DeviceIdType.MESH,
                )

    for load in loads[:3]:
        load.wait()
    pieces = jnp.concatenate(
        split_bf16(direction_ref[...], 3) + split_bf16(residual_ref[...], 3), axis=0
    )
    for q in range(rows):
        perm = perm_ref[q : q + 1, :]
        low = lax.bitwise_and(perm, 127)
        high = lax.shift_right_logical(perm, 7)
        onehot = (iota((128, 128), 0) == low).astype(f32).astype(bf16)
        onehot_ref[q] = onehot
        looked = dot_nn(pieces, onehot)
        mask = iota((rows, 128), 0) == high
        d_rows = (looked[0:rows] + looked[rows : 2 * rows]) + looked[2 * rows : 3 * rows]
        r_rows = (looked[3 * rows : 4 * rows] + looked[4 * rows : 5 * rows]) + looked[5 * rows :]
        c, k = q // pr, q % pr
        a_send[c, k : k + 1, :] = jnp.sum(jnp.where(mask, d_rows, 0.0), axis=0, keepdims=True)
        a_send[c, pr + k : pr + k + 1, :] = jnp.sum(
            jnp.where(mask, r_rows, 0.0), axis=0, keepdims=True
        )

    pl.semaphore_wait(barrier, T * RK - 1)

    a_recv[t] = a_send[t]
    for off in range(1, T):
        c = lax.rem(t + off, T)
        remote(a_send.at[c], a_recv.at[t], a_ss.at[c], a_rs.at[t], c, r).start()

    for load in loads[3:8]:
        load.wait()
    slots_ref[...] = jnp.zeros_like(slots_ref)
    slots_ref[0:1, 0:NBS] = target_ref[...]
    slots_ref[1:2, 0:NBS] = leaf_ref[...]
    diagonal = iota((NBP, 128), 0) == iota((NBP, 128), 1)
    target_row = slots_ref[0:1, :]
    leaf_row = slots_ref[1:2, :]
    target_col = jnp.sum(jnp.where(diagonal, target_row, 0), axis=1, keepdims=True)
    leaf_col = jnp.sum(jnp.where(diagonal, leaf_row, 0), axis=1, keepdims=True)
    live = iota((1, 128), 1) < live_smem[0]
    spread_hot = (
        ((iota((3 * gt, 128), 0) == lax.shift_right_logical(target_row, 1)) & live)
        .astype(f32)
        .astype(bf16)[:, :NBP]
    )
    pick_hot = (iota((NBP, 3 * gt), 1) == lax.shift_right_logical(target_col, 1)).astype(f32).astype(bf16)
    leaf_hot = (iota((NBP, rows), 1) == leaf_col).astype(f32).astype(bf16)
    leaf_spread = ((iota((rows, 128), 0) == leaf_row) & live).astype(f32).astype(bf16)[:, :NBP]
    odd = lax.bitwise_and(target_col, 1) == 1
    upper = iota((NBP, 128), 1) >= LD
    for k in range(KC):
        for g in range(G):
            weight_s[k * G + g : k * G + g + 1, :] = weight_ref[k : k + 1, g * 128 : (g + 1) * 128]
    values_s[...] = jnp.zeros_like(values_s)

    for off in range(1, T):
        s = lax.rem(t + off, T)
        remote(a_send.at[s], a_recv.at[s], a_ss.at[s], a_rs.at[s], s, r).wait_recv()
    for s in range(T):
        vec_f[s * pr : (s + 1) * pr, :] = a_recv[s, 0:pr, :]
        res_f[s * pr : (s + 1) * pr, :] = a_recv[s, pr : 2 * pr, :]

    vec_row = jnp.concatenate([vec_f[q : q + 1, :] for q in range(rows)], axis=1).astype(bf16)
    b_send[:, 0:WR] = dot_nt(vec_row, col_ref[...])

    def far(c):
        return jnp.abs(c - t) > 1

    for off in range(1, T):
        c = lax.rem(t + off, T)

        @pl.when(far(c))
        def _():
            for k in range(RK):
                remote(
                    b_send, b_recv.at[me], b_ss.at[c * RK + k], b_rs.at[me], c, k
                ).start()

    picked = dot_nn(leaf_hot, vec_f[...].astype(bf16)).astype(bf16)
    for b in range(NBS):
        values_s[b : b + 1, :] = dot_nt(
            picked[b : b + 1, :], blocks_ref[b * KI : (b + 1) * KI, :]
        )
    for k in range(KC):
        part = values_s[:, (k // 2) * 128 : (k // 2 + 1) * 128]
        rolled = pltpu.roll(part, LD, 1)
        moved = jnp.where(odd, rolled, part) if k % 2 == 0 else jnp.where(odd, part, rolled)
        moved = jnp.where(upper == odd, moved, 0.0)
        head, tail = split_bf16(moved, 2)
        summed = dot_nn(spread_hot, head) + dot_nn(spread_hot, tail)
        for o in range(3):
            for k2 in range(RK):
                start = o * gt + k2 * G
                c_send[o, k2, k * G : (k + 1) * G, :] = summed[start : start + G, :]
    for o in range(3):
        for k2 in range(RK):
            c_out = c_send[o, k2].astype(bf16)
            c_bf = c_out
            d_send[1 + o * RK + k2] = c_bf

    def inside(c):
        return (c >= 0) & (c < T)

    def near_copies(source, landing, ss, rs, mirrored, act):
        for o in (0, 2, 1):
            there = t + (1 - o if mirrored else o - 1)

            @pl.when(inside(there))
            def _():
                for dr in range(RK):
                    if o == 1 and dr == 0:
                        continue
                    k2 = lax.rem(r + dr, RK)
                    act(
                        remote(
                            source(o, k2), landing.at[o, r], ss.at[o, k2], rs.at[o, r], there, k2
                        )
                    )

    def near_waits(landing, ss, rs, mirrored):
        for o in (1, 0, 2):
            there = t + (o - 1 if mirrored else 1 - o)

            @pl.when(inside(there))
            def _():
                for dr in range(RK):
                    if o == 1 and dr == 0:
                        continue
                    k2 = lax.rem(r + dr, RK)
                    remote(
                        landing.at[o, k2], landing.at[o, k2], ss.at[o, k2], rs.at[o, k2], t, k2
                    ).wait_recv()

    def c_source(o, k2):
        return d_send.at[1 + o * RK + k2]

    def d_source(o, k2):
        return d_send.at[0]

    near_copies(c_source, c_recv, c_ss, c_rs, False, lambda copy: copy.start())

    loads[8].wait()
    loads[9].wait()
    for off in range(1, T):
        c = lax.rem(t + off, T)

        @pl.when(far(c))
        def _():
            for k in range(RK):
                slot = c * RK + k
                remote(b_send, b_recv.at[slot], b_ss.at[slot], b_rs.at[slot], c, k).wait_recv()

    far_coef = jnp.zeros((1, WR), f32)
    for c in range(T):
        coef = b_recv[c * RK]
        for k in range(1, RK):
            coef = coef + b_recv[c * RK + k]
        far_coef = far_coef + dot_nt(coef[:, 0:WR].astype(bf16), coupling_ref[c])
    far_bf = far_coef.astype(bf16)
    for k in range(KC):
        far_row = dot_nn(far_bf, row_ref[k])
        for g in range(G):
            far_s[k * G + g : k * G + g + 1, :] = far_row[:, g * 128 : (g + 1) * 128]

    near_waits(c_recv, c_ss, c_rs, False)
    own = jnp.zeros((KG, 128), f32)
    for k2 in range(RK):
        own = own + jnp.where(r == k2, c_send[1, k2], 0.0)
    near = own
    for o in range(3):
        for k2 in range(RK):
            near = near + c_recv[o, k2].astype(f32)
    weighted = (weight_s[...] * (far_s[...] + near)).astype(bf16)
    d_send[0] = weighted
    weighted_f[...] = weighted.astype(f32)
    near_copies(d_source, d_recv, d_ss, d_rs, True, lambda copy: copy.start())
    d_recv[1, r] = weighted

    back_part = jnp.zeros((1, WR), f32)
    for k in range(KC):
        weighted_row = jnp.concatenate(
            [weighted_f[k * G + g : k * G + g + 1, :] for g in range(G)], axis=1
        )
        back_part = back_part + dot_nt(weighted_row.astype(bf16), row_ref[k])
    back_two = jnp.concatenate(split_bf16(back_part, 2), axis=0)
    for c in range(T):
        two = dot_nn(back_two, coupling_ref[c])
        e_send[c, :, 0:WR] = two[0:1, :] + two[1:2, :]
    for off in range(1, T):
        c = lax.rem(t + off, T)

        @pl.when(far(c))
        def _():
            for k in range(RK):
                remote(
                    e_send.at[c], e_recv.at[me], e_ss.at[c * RK + k], e_rs.at[me], c, k
                ).start()

    near_waits(d_recv, d_ss, d_rs, True)
    chosen = []
    for k in range(KC):
        window = jnp.concatenate(
            [
                d_recv[o, k2, :, :].astype(f32)[k * G : (k + 1) * G, :]
                for o in range(3)
                for k2 in range(RK)
            ],
            axis=0,
        ).astype(bf16)
        found = dot_nn(pick_hot, window)
        rolled = pltpu.roll(found, LD, 1)
        chosen.append(
            jnp.where(odd, rolled, found) if k % 2 == 0 else jnp.where(odd, found, rolled)
        )
    chosen_rows = jnp.concatenate(
        [jnp.where(upper, chosen[2 * m + 1], chosen[2 * m]) for m in range(KC // 2)], axis=1
    ).astype(bf16)
    for b in range(NBS):
        values_s[b : b + 1, 0:128] = dot_nn(
            chosen_rows[b : b + 1, :], blocks_ref[b * KI : (b + 1) * KI, :]
        )
    head, tail = split_bf16(values_s[:, 0:128], 2)
    near_back = dot_nn(leaf_spread, head) + dot_nn(leaf_spread, tail)

    for off in range(1, T):
        c = lax.rem(t + off, T)

        @pl.when(far(c))
        def _():
            for k in range(RK):
                slot = c * RK + k
                remote(e_send.at[c], e_recv.at[slot], e_ss.at[slot], e_rs.at[slot], c, k).wait_recv()

    cluster_back = jnp.zeros((1, 128), f32)
    for slot in range(T * RK):
        cluster_back = cluster_back + e_recv[slot]
    far_back = dot_nn(cluster_back[:, 0:WR].astype(bf16), col_ref[...])
    for q in range(rows):
        far_back_s[q : q + 1, :] = far_back[:, q * 128 : (q + 1) * 128]
    image = far_back_s[...] + near_back
    for s in range(T):
        image_s[s] = image[s * pr : (s + 1) * pr, :]
    for off in range(1, T):
        s = lax.rem(t + off, T)
        remote(image_s.at[s], f_recv.at[t], f_ss.at[s], f_rs.at[t], s, r).start()
    f_recv[t] = image_s[t]

    vec = vec_f[...]
    res = res_f[...]
    normal = image + damping_weight * vec

    def total(x):
        return jnp.sum(jnp.sum(x, axis=0, keepdims=True), axis=1, keepdims=True)

    lane = iota((1, 128), 1)
    sums = jnp.where(lane == 0, total(vec * normal), 0.0)
    sums = jnp.where(lane == 1, total(res * normal), sums)
    sums = jnp.where(lane == 2, total(normal * normal), sums)
    sums = jnp.where(lane == 3, total(res * res), sums)
    g_send[...] = sums
    g_recv[me] = sums
    others = [(dt, dr) for dt in range(T) for dr in range(RK) if dt or dr]
    for dt, dr in others:
        c, k = lax.rem(t + dt, T), lax.rem(r + dr, RK)
        remote(g_send, g_recv.at[me], g_ss.at[c * RK + k], g_rs.at[me], c, k).start()

    for off in range(1, T):
        s = lax.rem(t + off, T)
        remote(image_s.at[s], f_recv.at[s], f_ss.at[s], f_rs.at[s], s, r).wait_recv()
    back = jnp.zeros((3 * rows, 128), f32)
    for q in range(rows):
        perm = perm_ref[q : q + 1, :]
        high = lax.shift_right_logical(perm, 7)
        mask = iota((rows, 128), 0) == high
        entry = f_recv[q // pr, q % pr : q % pr + 1, :]
        parts = split_bf16(jnp.where(mask, entry, 0.0), 3)
        back = back + dot_nt(jnp.concatenate(parts, axis=0), onehot_ref[q])
    slab = (back[0:rows] + back[rows : 2 * rows]) + back[2 * rows :]
    image_out[...] = slab + damping_weight * direction_ref[...]

    for dt, dr in others:
        c, k = lax.rem(t + dt, T), lax.rem(r + dr, RK)
        slot = c * RK + k
        remote(g_send, g_recv.at[slot], g_ss.at[slot], g_rs.at[slot], c, k).wait_recv()
    sums = g_recv[0]
    for slot in range(1, T * RK):
        sums = sums + g_recv[slot]

    def pick(i):
        return jnp.sum(jnp.where(lane == i, sums, 0.0), axis=1, keepdims=True)

    norm_now = pick(3) + tiny_value
    alpha = norm_now / (pick(0) + tiny_value)
    norm_next = pick(3) - 2.0 * alpha * pick(1) + alpha * alpha * pick(2)
    beta = jnp.maximum(norm_next, 0.0) / norm_now
    alpha_out[...] = jnp.broadcast_to(alpha, alpha_out.shape)
    beta_out[...] = jnp.broadcast_to(beta, beta_out.shape)

    for off in range(1, T):
        c = lax.rem(t + off, T)
        remote(a_send.at[c], a_recv.at[t], a_ss.at[c], a_rs.at[t], c, r).wait_send()
        remote(image_s.at[c], f_recv.at[t], f_ss.at[c], f_rs.at[t], c, r).wait_send()

        @pl.when(far(c))
        def _():
            for k in range(RK):
                remote(b_send, b_recv.at[me], b_ss.at[c * RK + k], b_rs.at[me], c, k).wait_send()
                remote(
                    e_send.at[c], e_recv.at[me], e_ss.at[c * RK + k], e_rs.at[me], c, k
                ).wait_send()

    near_copies(c_source, c_recv, c_ss, c_rs, False, lambda copy: copy.wait_send())
    near_copies(d_source, d_recv, d_ss, d_rs, True, lambda copy: copy.wait_send())
    for dt, dr in others:
        c, k = lax.rem(t + dt, T), lax.rem(r + dr, RK)
        remote(g_send, g_recv.at[me], g_ss.at[c * RK + k], g_rs.at[me], c, k).wait_send()


def fused(
    step_now,
    residual,
    direction,
    slab_perm,
    col_basis,
    row_basis,
    coupling,
    near_blocks,
    near_leaf,
    near_target,
    near_live,
    data_weight,
):
    T, RK = lax.axis_size("tile"), lax.axis_size("rank")
    N = T * RK
    rows = direction.shape[0] // 128
    pr = rows // T
    NBS, KC = near_blocks.shape[0], near_blocks.shape[1]
    WR = col_basis.shape[0]
    G = data_weight.shape[1] // 128
    KG = KC * G
    NBP = -(-NBS // 16) * 16
    f32, bf16 = jnp.float32, jnp.bfloat16
    res2 = residual.reshape(rows, 128)
    dir2 = direction.reshape(rows, 128)
    vmem = pl.BlockSpec(memory_space=pltpu.VMEM)
    hbm = pl.BlockSpec(memory_space=pltpu.HBM)
    row3 = row_basis.transpose(1, 0, 2)
    blocks2 = near_blocks.reshape(-1, LEAF)
    sem = pltpu.SemaphoreType.DMA
    out = jax.ShapeDtypeStruct((rows, 128), f32)
    image, alpha, beta = pl.pallas_call(
        functools.partial(cg_kernel, (T, RK, NBS, KC, WR)),
        out_shape=(out, out, out),
        in_specs=[hbm] * 9 + [pl.BlockSpec(memory_space=pltpu.SMEM), hbm],
        out_specs=(vmem, vmem, vmem),
        scratch_shapes=[
            pltpu.VMEM((rows, 128), f32),
            pltpu.VMEM((rows, 128), f32),
            pltpu.VMEM((rows, 128), jnp.int32),
            pltpu.VMEM((1, NBS), jnp.int32),
            pltpu.VMEM((1, NBS), jnp.int32),
            pltpu.VMEM(data_weight.shape, f32),
            pltpu.VMEM(col_basis.shape, bf16),
            pltpu.VMEM(row3.shape, bf16),
            pltpu.VMEM(coupling.shape[1:], bf16),
            pltpu.VMEM(blocks2.shape, bf16),
            pltpu.VMEM((rows, 128, 128), bf16),
            pltpu.VMEM((8, 128), jnp.int32),
            pltpu.VMEM((KG, 128), f32),
            pltpu.VMEM((KG, 128), f32),
            pltpu.VMEM((KG, 128), f32),
            pltpu.VMEM((T, 2 * pr, 128), f32),
            pltpu.VMEM((T, 2 * pr, 128), f32),
            pltpu.VMEM((rows, 128), f32),
            pltpu.VMEM((rows, 128), f32),
            pltpu.VMEM((1, 128), f32),
            pltpu.VMEM((N, 1, 128), f32),
            pltpu.VMEM((3, RK, KG, 128), f32),
            pltpu.VMEM((3, RK, KG, 128), bf16),
            pltpu.VMEM((1 + 3 * RK, KG, 128), bf16),
            pltpu.VMEM((3, RK, KG, 128), bf16),
            pltpu.VMEM((T, 1, 128), f32),
            pltpu.VMEM((N, 1, 128), f32),
            pltpu.VMEM((rows, 128), f32),
            pltpu.VMEM((T, pr, 128), f32),
            pltpu.VMEM((T, pr, 128), f32),
            pltpu.VMEM((1, 128), f32),
            pltpu.VMEM((N, 1, 128), f32),
            pltpu.VMEM((NBP, KC * LD), f32),
            sem((10,)),
            sem((T,)),
            sem((T,)),
            sem((N,)),
            sem((N,)),
            sem((3, RK)),
            sem((3, RK)),
            sem((3, RK)),
            sem((3, RK)),
            sem((N,)),
            sem((N,)),
            sem((T,)),
            sem((T,)),
            sem((N,)),
            sem((N,)),
        ],
        compiler_params=pltpu.CompilerParams(
            collective_id=0, has_side_effects=True, vmem_limit_bytes=64 * 1024 * 1024
        ),
    )(
        res2,
        dir2,
        slab_perm.reshape(rows, 128),
        col_basis,
        row3,
        coupling[0],
        blocks2,
        near_leaf.reshape(1, NBS),
        near_target.reshape(1, NBS),
        near_live,
        data_weight,
    )
    new_step = step_now.reshape(rows, 128) + alpha * dir2
    new_residual = res2 - alpha * image
    new_direction = new_residual + beta * dir2
    return tuple(x.reshape(-1) for x in (new_step, new_residual, new_direction))


def solution(mesh):
    def body(*args):
        piece = args[2].shape[0] // mesh.shape["tile"]
        return (per_device if piece % 128 else fused)(*args)

    return jax.shard_map(
        body,
        mesh=mesh,
        in_specs=(
            P(("tile", "rank")),
            P(("tile", "rank")),
            P(("tile", "rank")),
            P(("tile", "rank")),
            P(None, ("tile", "rank")),
            P(None, None, ("tile", "rank")),
            P("tile", None, None, None),
            P(("tile", "rank"), None, None, None),
            P(("tile", "rank")),
            P(("tile", "rank")),
            P(("tile", "rank")),
            P(None, ("tile", "rank")),
        ),
        out_specs=(P(("tile", "rank")), P(("tile", "rank")), P(("tile", "rank"))),
        check_vma=False,
    )
```

```python
import functools

import jax
import jax.numpy as jnp
from jax import lax
from jax.experimental import pallas as pl
from jax.experimental.pallas import tpu as pltpu
from jax.sharding import PartitionSpec as P

LEAF = 128
LD = 64


damping_weight = 0.5
tiny_value = 1e-06


def with_halo(block, sides, width):
    for axis, dim in sides:
        count = lax.axis_size(axis)
        forward = [(i, i + 1) for i in range(count - 1)]
        backward = [(target, source) for source, target in forward]
        low = lax.ppermute(
            lax.slice_in_dim(block, block.shape[dim] - width, None, axis=dim), axis, forward
        )
        high = lax.ppermute(lax.slice_in_dim(block, 0, width, axis=dim), axis, backward)
        block = jnp.concatenate([low, block, high], axis=dim)
    return block


def per_device(
    step_now,
    residual,
    direction,
    slab_perm,
    col_basis,
    row_basis,
    coupling,
    near_blocks,
    near_leaf,
    near_target,
    near_live,
    data_weight,
):
    tile_count = lax.axis_size("tile")
    rank_count = lax.axis_size("rank")
    tile_here = lax.axis_index("tile")
    slab_len = direction.shape[0]
    piece_len = slab_len // tile_count
    tile_points = data_weight.shape[1] * rank_count
    data_leaves = tile_points // LD
    leaf_count = slab_len // LEAF
    width_rank = col_basis.shape[0]
    block_slots = near_blocks.shape[0]
    dir_bf = direction.astype(jnp.bfloat16)
    outgoing = dir_bf[slab_perm].reshape(tile_count, piece_len)
    cluster_vec = lax.all_to_all(outgoing, "tile", split_axis=0, concat_axis=0, tiled=True).reshape(
        slab_len
    )
    coef_part = jnp.dot(col_basis, cluster_vec, preferred_element_type=jnp.float32)
    coef_all = lax.all_gather(coef_part[None, :], ("tile", "rank"), axis=0, tiled=True)
    cluster_coef = (
        coef_all.reshape(tile_count, rank_count, width_rank).sum(axis=1).astype(jnp.bfloat16)
    )
    far_keep = jnp.abs(jnp.arange(tile_count, dtype=jnp.int32) - tile_here) > 1
    masked_coef = cluster_coef * far_keep[:, None].astype(jnp.bfloat16)
    far_coef = jnp.einsum(
        "cab,cb->a", coupling[0], masked_coef, preferred_element_type=jnp.float32
    ).astype(jnp.bfloat16)
    basis_flat = row_basis.reshape(width_rank, -1)
    far_data = jnp.dot(far_coef, basis_flat, preferred_element_type=jnp.float32).reshape(6, -1)
    live_mask = jnp.arange(block_slots, dtype=jnp.int32) < near_live[0]
    offset = near_target // data_leaves
    data_leaf = near_target % data_leaves
    picked = cluster_vec.reshape(leaf_count, LEAF)[near_leaf]
    values = jnp.einsum("bkij,bj->bki", near_blocks, picked, preferred_element_type=jnp.float32)
    values = values * live_mask[:, None, None].astype(jnp.float32)
    partial_value = (
        jnp.zeros((3, 6, data_leaves, LD), jnp.float32).at[offset, :, data_leaf, :].add(values)
    )
    partial_value = partial_value.reshape(3, 6, tile_points)
    shares = lax.psum_scatter(partial_value, "rank", scatter_dimension=2, tiled=True)
    edges = jnp.stack([shares[0], shares[2]])
    extended = with_halo(edges, (("tile", 0),), 1)
    near_data = shares[1] + extended[0] + extended[3]
    weighted = (data_weight * (far_data + near_data)).astype(jnp.bfloat16)
    back_part = jnp.dot(basis_flat, weighted.reshape(-1), preferred_element_type=jnp.float32)
    back_coef = lax.psum(back_part, "rank").astype(jnp.bfloat16)
    spread = jnp.einsum("cab,a->cb", coupling[0], back_coef, preferred_element_type=jnp.float32)
    spread = spread * far_keep[:, None].astype(jnp.float32)
    cluster_back = lax.psum_scatter(spread, "tile", scatter_dimension=0, tiled=True).astype(
        jnp.bfloat16
    )
    far_back = jnp.dot(cluster_back[0], col_basis, preferred_element_type=jnp.float32)
    tile_data = lax.all_gather(weighted, "rank", axis=1, tiled=True)
    window = with_halo(tile_data[None], (("tile", 0),), 1)
    chosen = window.reshape(3, 6, data_leaves, LD)[offset, :, data_leaf, :]
    back_values = jnp.einsum(
        "bkij,bki->bj", near_blocks, chosen, preferred_element_type=jnp.float32
    )
    back_values = back_values * live_mask[:, None].astype(jnp.float32)
    near_back = (
        jnp.zeros((leaf_count, LEAF), jnp.float32).at[near_leaf].add(back_values).reshape(slab_len)
    )
    cluster_image = far_back + near_back
    returned = lax.all_to_all(
        cluster_image.reshape(tile_count, piece_len),
        "tile",
        split_axis=0,
        concat_axis=0,
        tiled=True,
    ).reshape(slab_len)
    slab_image = jnp.zeros((slab_len,), jnp.float32).at[slab_perm].set(returned)
    normal_image = slab_image + damping_weight * direction
    norm_now, curvature = lax.psum(
        (jnp.sum(residual * residual), jnp.sum(direction * normal_image)), ("tile", "rank")
    )
    norm_now = norm_now + tiny_value
    step_size = norm_now / (curvature + tiny_value)
    new_step = step_now + step_size * direction
    new_residual = residual - step_size * normal_image
    norm_next = lax.psum(jnp.sum(new_residual * new_residual), ("tile", "rank"))
    new_direction = new_residual + norm_next / norm_now * direction
    return (new_step, new_residual, new_direction)


def split_bf16(x, parts):
    out = []
    for _ in range(parts):
        head = x.astype(jnp.bfloat16)
        out.append(head)
        x = x - head.astype(jnp.float32)
    return out


def dot_nt(a, b):
    return lax.dot_general(a, b, (((1,), (1,)), ((), ())), preferred_element_type=jnp.float32)


def dot_nn(a, b):
    return jnp.dot(a, b, preferred_element_type=jnp.float32)


def iota(shape, dim):
    return lax.broadcasted_iota(jnp.int32, shape, dim)


def cg_kernel(
    dims,
    residual_hbm,
    direction_hbm,
    perm_hbm,
    col_hbm,
    row_hbm,
    coupling_hbm,
    blocks_hbm,
    leaf_hbm,
    target_hbm,
    live_smem,
    weight_hbm,
    image_out,
    alpha_out,
    beta_out,
    residual_ref,
    direction_ref,
    perm_ref,
    leaf_ref,
    target_ref,
    weight_ref,
    col_ref,
    row_ref,
    coupling_ref,
    blocks_ref,
    onehot_ref,
    slots_ref,
    weight_s,
    far_s,
    weighted_f,
    a_send,
    a_recv,
    vec_f,
    res_f,
    b_send,
    b_recv,
    b_all,
    c_send,
    c_recv,
    d_send,
    d_recv,
    e_send,
    e_recv,
    e_sum,
    e_all,
    far_back_s,
    image_s,
    f_recv,
    g_send,
    g_all,
    values_s,
    load_sem,
    a_ss,
    a_rs,
    b_ss,
    b_rs,
    b2_ss,
    b2_rs,
    c_ss,
    c_rs,
    d_ss,
    d_rs,
    e_ss,
    e_rs,
    e2_ss,
    e2_rs,
    f_ss,
    f_rs,
    g_ss,
    g_rs,
):
    T, RK, NBS, KC, WR = dims
    bf16, f32 = jnp.bfloat16, jnp.float32
    rows = direction_hbm.shape[0]
    pr = rows // T
    G = weight_hbm.shape[1] // 128
    KG = KC * G
    gt = G * RK
    NBP = values_s.shape[0]
    KI = KC * LD
    t = lax.axis_index("tile")
    r = lax.axis_index("rank")

    def remote(src, dst, ss, rs, tile, rank):
        return pltpu.make_async_remote_copy(
            src_ref=src,
            dst_ref=dst,
            send_sem=ss,
            recv_sem=rs,
            device_id=(tile, rank),
            device_id_type=pl.DeviceIdType.MESH,
        )

    def inside(c):
        return (c >= 0) & (c < T)

    def far(c):
        return jnp.abs(c - t) > 1

    def rank_copies(source, landing, ss, rs):
        peers = [lax.rem(r + dr, RK) for dr in range(1, RK)]
        return [remote(source, landing.at[r], ss.at[k], rs.at[r], t, k) for k in peers]

    def rank_waits(landing, ss, rs):
        for dr in range(1, RK):
            k = lax.rem(r + dr, RK)
            remote(landing.at[k], landing.at[k], ss.at[k], rs.at[k], t, k).wait_recv()

    operands = [
        (direction_hbm, direction_ref),
        (perm_hbm, perm_ref),
        (residual_hbm, residual_ref),
        (leaf_hbm, leaf_ref),
        (target_hbm, target_ref),
        (weight_hbm, weight_ref),
        (col_hbm, col_ref),
        (blocks_hbm, blocks_ref),
        (coupling_hbm, coupling_ref),
        (row_hbm, row_ref),
    ]
    loads = [
        pltpu.make_async_copy(source, held, load_sem.at[i])
        for i, (source, held) in enumerate(operands)
    ]
    for load in loads:
        load.start()

    b_recv[...] = jnp.zeros_like(b_recv)
    e_recv[...] = jnp.zeros_like(e_recv)
    c_recv[...] = jnp.zeros_like(c_recv)
    d_recv[...] = jnp.zeros_like(d_recv)

    barrier = pltpu.get_barrier_semaphore()

    def greet(tile, rank):
        pl.semaphore_signal(
            barrier, inc=1, device_id=(tile, rank), device_id_type=pl.DeviceIdType.MESH
        )

    for dt in range(1, T):
        greet(lax.rem(t + dt, T), r)
    for dr in range(1, RK):
        greet(t, lax.rem(r + dr, RK))
    for side in (-1, 1):

        @pl.when(inside(t + side))
        def _():
            for dr in range(1, RK):
                greet(t + side, lax.rem(r + dr, RK))

    sides = jnp.where(t > 0, 1, 0) + jnp.where(t < T - 1, 1, 0)

    for load in loads[:3]:
        load.wait()
    pieces = jnp.concatenate(
        split_bf16(direction_ref[...], 3) + split_bf16(residual_ref[...], 3), axis=0
    )
    for q in range(rows):
        perm = perm_ref[q : q + 1, :]
        low = lax.bitwise_and(perm, 127)
        high = lax.shift_right_logical(perm, 7)
        onehot = (iota((128, 128), 0) == low).astype(f32).astype(bf16)
        onehot_ref[q] = onehot
        looked = dot_nn(pieces, onehot)
        mask = iota((rows, 128), 0) == high
        d_rows = (looked[0:rows] + looked[rows : 2 * rows]) + looked[2 * rows : 3 * rows]
        r_rows = (looked[3 * rows : 4 * rows] + looked[4 * rows : 5 * rows]) + looked[5 * rows :]
        c, k = q // pr, q % pr
        a_send[c, k : k + 1, :] = jnp.sum(jnp.where(mask, d_rows, 0.0), axis=0, keepdims=True)
        a_send[c, pr + k : pr + k + 1, :] = jnp.sum(
            jnp.where(mask, r_rows, 0.0), axis=0, keepdims=True
        )

    pl.semaphore_wait(barrier, T - 1 + (RK - 1) * (1 + sides))

    a_recv[t] = a_send[t]
    for off in range(1, T):
        c = lax.rem(t + off, T)
        remote(a_send.at[c], a_recv.at[t], a_ss.at[c], a_rs.at[t], c, r).start()

    for load in loads[3:8]:
        load.wait()
    slots_ref[...] = jnp.zeros_like(slots_ref)
    slots_ref[0:1, 0:NBS] = target_ref[...]
    slots_ref[1:2, 0:NBS] = leaf_ref[...]
    diagonal = iota((NBP, 128), 0) == iota((NBP, 128), 1)
    target_row = slots_ref[0:1, :]
    leaf_row = slots_ref[1:2, :]
    target_col = jnp.sum(jnp.where(diagonal, target_row, 0), axis=1, keepdims=True)
    leaf_col = jnp.sum(jnp.where(diagonal, leaf_row, 0), axis=1, keepdims=True)
    live = iota((1, 128), 1) < live_smem[0]
    spread_hot = (
        ((iota((3 * gt, 128), 0) == lax.shift_right_logical(target_row, 1)) & live)
        .astype(f32)
        .astype(bf16)[:, :NBP]
    )
    pick_hot = (iota((NBP, 3 * gt), 1) == lax.shift_right_logical(target_col, 1)).astype(f32).astype(bf16)
    leaf_hot = (iota((NBP, rows), 1) == leaf_col).astype(f32).astype(bf16)
    leaf_spread = ((iota((rows, 128), 0) == leaf_row) & live).astype(f32).astype(bf16)[:, :NBP]
    odd = lax.bitwise_and(target_col, 1) == 1
    upper = iota((NBP, 128), 1) >= LD
    for k in range(KC):
        for g in range(G):
            weight_s[k * G + g : k * G + g + 1, :] = weight_ref[k : k + 1, g * 128 : (g + 1) * 128]
    values_s[...] = jnp.zeros_like(values_s)

    for off in range(1, T):
        s = lax.rem(t + off, T)
        remote(a_send.at[s], a_recv.at[s], a_ss.at[s], a_rs.at[s], s, r).wait_recv()
    for s in range(T):
        vec_f[s * pr : (s + 1) * pr, :] = a_recv[s, 0:pr, :]
        res_f[s * pr : (s + 1) * pr, :] = a_recv[s, pr : 2 * pr, :]

    vec_row = jnp.concatenate([vec_f[q : q + 1, :] for q in range(rows)], axis=1).astype(bf16)
    b_send[:, 0:WR] = dot_nt(vec_row, col_ref[...])

    for off in range(1, T):
        c = lax.rem(t + off, T)

        @pl.when(far(c))
        def _():
            remote(b_send, b_recv.at[t], b_ss.at[c], b_rs.at[t], c, r).start()

    picked = dot_nn(leaf_hot, vec_f[...].astype(bf16)).astype(bf16)
    for b in range(NBS):
        values_s[b : b + 1, :] = dot_nt(
            picked[b : b + 1, :], blocks_ref[b * KI : (b + 1) * KI, :]
        )
    for off in range(1, T):
        c = lax.rem(t + off, T)

        @pl.when(far(c))
        def _():
            remote(b_send, b_recv.at[c], b_ss.at[c], b_rs.at[c], c, r).wait_recv()

    for copy in rank_copies(b_recv, b_all, b2_ss, b2_rs):
        copy.start()
    b_all[r] = b_recv[...]
    for k in range(KC):
        part = values_s[:, (k // 2) * 128 : (k // 2 + 1) * 128]
        rolled = pltpu.roll(part, LD, 1)
        moved = jnp.where(odd, rolled, part) if k % 2 == 0 else jnp.where(odd, part, rolled)
        moved = jnp.where(upper == odd, moved, 0.0)
        head, tail = split_bf16(moved, 2)
        summed = dot_nn(spread_hot, head) + dot_nn(spread_hot, tail)
        for o in range(3):
            for k2 in range(RK):
                start = o * gt + k2 * G
                c_send[o, k2, k * G : (k + 1) * G, :] = summed[start : start + G, :]
    for o in range(3):
        for k2 in range(RK):
            c_out = c_send[o, k2].astype(bf16)
            c_bf = c_out
            d_send[1 + o * RK + k2] = c_bf

    def near_copies(source, landing, ss, rs, mirrored, act):
        for o in (0, 2, 1):
            there = t + (1 - o if mirrored else o - 1)

            @pl.when(inside(there))
            def _():
                for dr in range(RK):
                    if o == 1 and dr == 0:
                        continue
                    k2 = lax.rem(r + dr, RK)
                    act(
                        remote(
                            source(o, k2), landing.at[o, r], ss.at[o, k2], rs.at[o, r], there, k2
                        )
                    )

    def near_waits(landing, ss, rs, mirrored):
        for o in (1, 0, 2):
            there = t + (o - 1 if mirrored else 1 - o)

            @pl.when(inside(there))
            def _():
                for dr in range(RK):
                    if o == 1 and dr == 0:
                        continue
                    k2 = lax.rem(r + dr, RK)
                    remote(
                        landing.at[o, k2], landing.at[o, k2], ss.at[o, k2], rs.at[o, k2], t, k2
                    ).wait_recv()

    def c_source(o, k2):
        return d_send.at[1 + o * RK + k2]

    def d_source(o, k2):
        return d_send.at[0]

    near_copies(c_source, c_recv, c_ss, c_rs, False, lambda copy: copy.start())

    loads[8].wait()
    loads[9].wait()
    rank_waits(b_all, b2_ss, b2_rs)
    far_coef = jnp.zeros((1, WR), f32)
    for c in range(T):
        coef = b_all[0, c]
        for k in range(1, RK):
            coef = coef + b_all[k, c]
        far_coef = far_coef + dot_nt(coef[:, 0:WR].astype(bf16), coupling_ref[c])
    far_bf = far_coef.astype(bf16)
    for k in range(KC):
        far_row = dot_nn(far_bf, row_ref[k])
        for g in range(G):
            far_s[k * G + g : k * G + g + 1, :] = far_row[:, g * 128 : (g + 1) * 128]

    near_waits(c_recv, c_ss, c_rs, False)
    own = jnp.zeros((KG, 128), f32)
    for k2 in range(RK):
        own = own + jnp.where(r == k2, c_send[1, k2], 0.0)
    near = own
    for o in range(3):
        for k2 in range(RK):
            near = near + c_recv[o, k2].astype(f32)
    weighted = (weight_s[...] * (far_s[...] + near)).astype(bf16)
    d_send[0] = weighted
    weighted_f[...] = weighted.astype(f32)
    near_copies(d_source, d_recv, d_ss, d_rs, True, lambda copy: copy.start())
    d_recv[1, r] = weighted

    back_part = jnp.zeros((1, WR), f32)
    for k in range(KC):
        weighted_row = jnp.concatenate(
            [weighted_f[k * G + g : k * G + g + 1, :] for g in range(G)], axis=1
        )
        back_part = back_part + dot_nt(weighted_row.astype(bf16), row_ref[k])
    back_two = jnp.concatenate(split_bf16(back_part, 2), axis=0)
    for c in range(T):
        two = dot_nn(back_two, coupling_ref[c])
        e_send[c, :, 0:WR] = two[0:1, :] + two[1:2, :]
    for off in range(1, T):
        c = lax.rem(t + off, T)

        @pl.when(far(c))
        def _():
            remote(e_send.at[c], e_recv.at[t], e_ss.at[c], e_rs.at[t], c, r).start()

    near_waits(d_recv, d_ss, d_rs, True)
    for off in range(1, T):
        c = lax.rem(t + off, T)

        @pl.when(far(c))
        def _():
            remote(e_send.at[c], e_recv.at[c], e_ss.at[c], e_rs.at[c], c, r).wait_recv()

    spread_sum = e_recv[0]
    for c in range(1, T):
        spread_sum = spread_sum + e_recv[c]
    e_sum[...] = spread_sum
    for copy in rank_copies(e_sum, e_all, e2_ss, e2_rs):
        copy.start()
    e_all[r] = spread_sum
    chosen = []
    for k in range(KC):
        window = jnp.concatenate(
            [
                d_recv[o, k2, :, :].astype(f32)[k * G : (k + 1) * G, :]
                for o in range(3)
                for k2 in range(RK)
            ],
            axis=0,
        ).astype(bf16)
        found = dot_nn(pick_hot, window)
        rolled = pltpu.roll(found, LD, 1)
        chosen.append(
            jnp.where(odd, rolled, found) if k % 2 == 0 else jnp.where(odd, found, rolled)
        )
    chosen_rows = jnp.concatenate(
        [jnp.where(upper, chosen[2 * m + 1], chosen[2 * m]) for m in range(KC // 2)], axis=1
    ).astype(bf16)
    for b in range(NBS):
        values_s[b : b + 1, 0:128] = dot_nn(
            chosen_rows[b : b + 1, :], blocks_ref[b * KI : (b + 1) * KI, :]
        )
    head, tail = split_bf16(values_s[:, 0:128], 2)
    near_back = dot_nn(leaf_spread, head) + dot_nn(leaf_spread, tail)

    rank_waits(e_all, e2_ss, e2_rs)
    cluster_back = jnp.zeros((1, 128), f32)
    for k in range(RK):
        cluster_back = cluster_back + e_all[k]
    far_back = dot_nn(cluster_back[:, 0:WR].astype(bf16), col_ref[...])
    for q in range(rows):
        far_back_s[q : q + 1, :] = far_back[:, q * 128 : (q + 1) * 128]
    image = far_back_s[...] + near_back

    vec = vec_f[...]
    res = res_f[...]
    normal = image + damping_weight * vec

    def total(x):
        return jnp.sum(jnp.sum(x, axis=0, keepdims=True), axis=1, keepdims=True)

    lane = iota((1, 128), 1)
    sums = jnp.where(lane == 0, total(vec * normal), 0.0)
    sums = jnp.where(lane == 1, total(res * normal), sums)
    sums = jnp.where(lane == 2, total(normal * normal), sums)
    sums = jnp.where(lane == 3, total(res * res), sums)
    for s in range(T):
        image_s[s, 0:pr, :] = image[s * pr : (s + 1) * pr, :]
        image_s[s, pr : 2 * pr, :] = jnp.broadcast_to(sums, (pr, 128))
    for off in range(1, T):
        s = lax.rem(t + off, T)
        remote(image_s.at[s], f_recv.at[t], f_ss.at[s], f_rs.at[t], s, r).start()
    f_recv[t] = image_s[t]
    for off in range(1, T):
        s = lax.rem(t + off, T)
        remote(image_s.at[s], f_recv.at[s], f_ss.at[s], f_rs.at[s], s, r).wait_recv()
    tile_sums = f_recv[0, pr : pr + 1, :]
    for s in range(1, T):
        tile_sums = tile_sums + f_recv[s, pr : pr + 1, :]
    g_send[...] = tile_sums
    for copy in rank_copies(g_send, g_all, g_ss, g_rs):
        copy.start()
    g_all[r] = tile_sums
    back = jnp.zeros((3 * rows, 128), f32)
    for q in range(rows):
        perm = perm_ref[q : q + 1, :]
        high = lax.shift_right_logical(perm, 7)
        mask = iota((rows, 128), 0) == high
        entry = f_recv[q // pr, q % pr : q % pr + 1, :]
        parts = split_bf16(jnp.where(mask, entry, 0.0), 3)
        back = back + dot_nt(jnp.concatenate(parts, axis=0), onehot_ref[q])
    slab = (back[0:rows] + back[rows : 2 * rows]) + back[2 * rows :]
    image_out[...] = slab + damping_weight * direction_ref[...]

    rank_waits(g_all, g_ss, g_rs)
    sums = g_all[0]
    for k in range(1, RK):
        sums = sums + g_all[k]

    def pick(i):
        return jnp.sum(jnp.where(lane == i, sums, 0.0), axis=1, keepdims=True)

    norm_now = pick(3) + tiny_value
    alpha = norm_now / (pick(0) + tiny_value)
    norm_next = pick(3) - 2.0 * alpha * pick(1) + alpha * alpha * pick(2)
    beta = jnp.maximum(norm_next, 0.0) / norm_now
    alpha_out[...] = jnp.broadcast_to(alpha, alpha_out.shape)
    beta_out[...] = jnp.broadcast_to(beta, beta_out.shape)

    for off in range(1, T):
        c = lax.rem(t + off, T)
        remote(a_send.at[c], a_recv.at[t], a_ss.at[c], a_rs.at[t], c, r).wait_send()
        remote(image_s.at[c], f_recv.at[t], f_ss.at[c], f_rs.at[t], c, r).wait_send()

        @pl.when(far(c))
        def _():
            remote(b_send, b_recv.at[t], b_ss.at[c], b_rs.at[t], c, r).wait_send()
            remote(e_send.at[c], e_recv.at[t], e_ss.at[c], e_rs.at[t], c, r).wait_send()

    near_copies(c_source, c_recv, c_ss, c_rs, False, lambda copy: copy.wait_send())
    near_copies(d_source, d_recv, d_ss, d_rs, True, lambda copy: copy.wait_send())
    for copies in (
        rank_copies(b_recv, b_all, b2_ss, b2_rs),
        rank_copies(e_sum, e_all, e2_ss, e2_rs),
        rank_copies(g_send, g_all, g_ss, g_rs),
    ):
        for copy in copies:
            copy.wait_send()


def fused(
    step_now,
    residual,
    direction,
    slab_perm,
    col_basis,
    row_basis,
    coupling,
    near_blocks,
    near_leaf,
    near_target,
    near_live,
    data_weight,
):
    T, RK = lax.axis_size("tile"), lax.axis_size("rank")
    rows = direction.shape[0] // 128
    pr = rows // T
    NBS, KC = near_blocks.shape[0], near_blocks.shape[1]
    WR = col_basis.shape[0]
    G = data_weight.shape[1] // 128
    KG = KC * G
    NBP = -(-NBS // 16) * 16
    f32, bf16 = jnp.float32, jnp.bfloat16
    res2 = residual.reshape(rows, 128)
    dir2 = direction.reshape(rows, 128)
    vmem = pl.BlockSpec(memory_space=pltpu.VMEM)
    hbm = pl.BlockSpec(memory_space=pltpu.HBM)
    row3 = row_basis.transpose(1, 0, 2)
    blocks2 = near_blocks.reshape(-1, LEAF)
    sem = pltpu.SemaphoreType.DMA
    out = jax.ShapeDtypeStruct((rows, 128), f32)
    image, alpha, beta = pl.pallas_call(
        functools.partial(cg_kernel, (T, RK, NBS, KC, WR)),
        out_shape=(out, out, out),
        in_specs=[hbm] * 9 + [pl.BlockSpec(memory_space=pltpu.SMEM), hbm],
        out_specs=(vmem, vmem, vmem),
        scratch_shapes=[
            pltpu.VMEM((rows, 128), f32),
            pltpu.VMEM((rows, 128), f32),
            pltpu.VMEM((rows, 128), jnp.int32),
            pltpu.VMEM((1, NBS), jnp.int32),
            pltpu.VMEM((1, NBS), jnp.int32),
            pltpu.VMEM(data_weight.shape, f32),
            pltpu.VMEM(col_basis.shape, bf16),
            pltpu.VMEM(row3.shape, bf16),
            pltpu.VMEM(coupling.shape[1:], bf16),
            pltpu.VMEM(blocks2.shape, bf16),
            pltpu.VMEM((rows, 128, 128), bf16),
            pltpu.VMEM((8, 128), jnp.int32),
            pltpu.VMEM((KG, 128), f32),
            pltpu.VMEM((KG, 128), f32),
            pltpu.VMEM((KG, 128), f32),
            pltpu.VMEM((T, 2 * pr, 128), f32),
            pltpu.VMEM((T, 2 * pr, 128), f32),
            pltpu.VMEM((rows, 128), f32),
            pltpu.VMEM((rows, 128), f32),
            pltpu.VMEM((1, 128), f32),
            pltpu.VMEM((T, 1, 128), f32),
            pltpu.VMEM((RK, T, 1, 128), f32),
            pltpu.VMEM((3, RK, KG, 128), f32),
            pltpu.VMEM((3, RK, KG, 128), bf16),
            pltpu.VMEM((1 + 3 * RK, KG, 128), bf16),
            pltpu.VMEM((3, RK, KG, 128), bf16),
            pltpu.VMEM((T, 1, 128), f32),
            pltpu.VMEM((T, 1, 128), f32),
            pltpu.VMEM((1, 128), f32),
            pltpu.VMEM((RK, 1, 128), f32),
            pltpu.VMEM((rows, 128), f32),
            pltpu.VMEM((T, 2 * pr, 128), f32),
            pltpu.VMEM((T, 2 * pr, 128), f32),
            pltpu.VMEM((1, 128), f32),
            pltpu.VMEM((RK, 1, 128), f32),
            pltpu.VMEM((NBP, KC * LD), f32),
            sem((10,)),
            sem((T,)),
            sem((T,)),
            sem((T,)),
            sem((T,)),
            sem((RK,)),
            sem((RK,)),
            sem((3, RK)),
            sem((3, RK)),
            sem((3, RK)),
            sem((3, RK)),
            sem((T,)),
            sem((T,)),
            sem((RK,)),
            sem((RK,)),
            sem((T,)),
            sem((T,)),
            sem((RK,)),
            sem((RK,)),
        ],
        compiler_params=pltpu.CompilerParams(
            collective_id=0, has_side_effects=True, vmem_limit_bytes=64 * 1024 * 1024
        ),
    )(
        res2,
        dir2,
        slab_perm.reshape(rows, 128),
        col_basis,
        row3,
        coupling[0],
        blocks2,
        near_leaf.reshape(1, NBS),
        near_target.reshape(1, NBS),
        near_live,
        data_weight,
    )
    new_step = step_now.reshape(rows, 128) + alpha * dir2
    new_residual = res2 - alpha * image
    new_direction = new_residual + beta * dir2
    return tuple(x.reshape(-1) for x in (new_step, new_residual, new_direction))


def solution(mesh):
    def body(*args):
        piece = args[2].shape[0] // mesh.shape["tile"]
        return (per_device if piece % 128 else fused)(*args)

    return jax.shard_map(
        body,
        mesh=mesh,
        in_specs=(
            P(("tile", "rank")),
            P(("tile", "rank")),
            P(("tile", "rank")),
            P(("tile", "rank")),
            P(None, ("tile", "rank")),
            P(None, None, ("tile", "rank")),
            P("tile", None, None, None),
            P(("tile", "rank"), None, None, None),
            P(("tile", "rank")),
            P(("tile", "rank")),
            P(("tile", "rank")),
            P(None, ("tile", "rank")),
        ),
        out_specs=(P(("tile", "rank")), P(("tile", "rank")), P(("tile", "rank"))),
        check_vma=False,
    )
```

```python
import functools

import jax
import jax.numpy as jnp
from jax import lax
from jax.experimental import pallas as pl
from jax.experimental.pallas import tpu as pltpu
from jax.sharding import PartitionSpec as P

LEAF = 128
LD = 64


damping_weight = 0.5
tiny_value = 1e-06


def with_halo(block, sides, width):
    for axis, dim in sides:
        count = lax.axis_size(axis)
        forward = [(i, i + 1) for i in range(count - 1)]
        backward = [(target, source) for source, target in forward]
        low = lax.ppermute(
            lax.slice_in_dim(block, block.shape[dim] - width, None, axis=dim), axis, forward
        )
        high = lax.ppermute(lax.slice_in_dim(block, 0, width, axis=dim), axis, backward)
        block = jnp.concatenate([low, block, high], axis=dim)
    return block


def per_device(
    step_now,
    residual,
    direction,
    slab_perm,
    col_basis,
    row_basis,
    coupling,
    near_blocks,
    near_leaf,
    near_target,
    near_live,
    data_weight,
):
    tile_count = lax.axis_size("tile")
    rank_count = lax.axis_size("rank")
    tile_here = lax.axis_index("tile")
    slab_len = direction.shape[0]
    piece_len = slab_len // tile_count
    tile_points = data_weight.shape[1] * rank_count
    data_leaves = tile_points // LD
    leaf_count = slab_len // LEAF
    width_rank = col_basis.shape[0]
    block_slots = near_blocks.shape[0]
    dir_bf = direction.astype(jnp.bfloat16)
    outgoing = dir_bf[slab_perm].reshape(tile_count, piece_len)
    cluster_vec = lax.all_to_all(outgoing, "tile", split_axis=0, concat_axis=0, tiled=True).reshape(
        slab_len
    )
    coef_part = jnp.dot(col_basis, cluster_vec, preferred_element_type=jnp.float32)
    coef_all = lax.all_gather(coef_part[None, :], ("tile", "rank"), axis=0, tiled=True)
    cluster_coef = (
        coef_all.reshape(tile_count, rank_count, width_rank).sum(axis=1).astype(jnp.bfloat16)
    )
    far_keep = jnp.abs(jnp.arange(tile_count, dtype=jnp.int32) - tile_here) > 1
    masked_coef = cluster_coef * far_keep[:, None].astype(jnp.bfloat16)
    far_coef = jnp.einsum(
        "cab,cb->a", coupling[0], masked_coef, preferred_element_type=jnp.float32
    ).astype(jnp.bfloat16)
    basis_flat = row_basis.reshape(width_rank, -1)
    far_data = jnp.dot(far_coef, basis_flat, preferred_element_type=jnp.float32).reshape(6, -1)
    live_mask = jnp.arange(block_slots, dtype=jnp.int32) < near_live[0]
    offset = near_target // data_leaves
    data_leaf = near_target % data_leaves
    picked = cluster_vec.reshape(leaf_count, LEAF)[near_leaf]
    values = jnp.einsum("bkij,bj->bki", near_blocks, picked, preferred_element_type=jnp.float32)
    values = values * live_mask[:, None, None].astype(jnp.float32)
    partial_value = (
        jnp.zeros((3, 6, data_leaves, LD), jnp.float32).at[offset, :, data_leaf, :].add(values)
    )
    partial_value = partial_value.reshape(3, 6, tile_points)
    shares = lax.psum_scatter(partial_value, "rank", scatter_dimension=2, tiled=True)
    edges = jnp.stack([shares[0], shares[2]])
    extended = with_halo(edges, (("tile", 0),), 1)
    near_data = shares[1] + extended[0] + extended[3]
    weighted = (data_weight * (far_data + near_data)).astype(jnp.bfloat16)
    back_part = jnp.dot(basis_flat, weighted.reshape(-1), preferred_element_type=jnp.float32)
    back_coef = lax.psum(back_part, "rank").astype(jnp.bfloat16)
    spread = jnp.einsum("cab,a->cb", coupling[0], back_coef, preferred_element_type=jnp.float32)
    spread = spread * far_keep[:, None].astype(jnp.float32)
    cluster_back = lax.psum_scatter(spread, "tile", scatter_dimension=0, tiled=True).astype(
        jnp.bfloat16
    )
    far_back = jnp.dot(cluster_back[0], col_basis, preferred_element_type=jnp.float32)
    tile_data = lax.all_gather(weighted, "rank", axis=1, tiled=True)
    window = with_halo(tile_data[None], (("tile", 0),), 1)
    chosen = window.reshape(3, 6, data_leaves, LD)[offset, :, data_leaf, :]
    back_values = jnp.einsum(
        "bkij,bki->bj", near_blocks, chosen, preferred_element_type=jnp.float32
    )
    back_values = back_values * live_mask[:, None].astype(jnp.float32)
    near_back = (
        jnp.zeros((leaf_count, LEAF), jnp.float32).at[near_leaf].add(back_values).reshape(slab_len)
    )
    cluster_image = far_back + near_back
    returned = lax.all_to_all(
        cluster_image.reshape(tile_count, piece_len),
        "tile",
        split_axis=0,
        concat_axis=0,
        tiled=True,
    ).reshape(slab_len)
    slab_image = jnp.zeros((slab_len,), jnp.float32).at[slab_perm].set(returned)
    normal_image = slab_image + damping_weight * direction
    norm_now, curvature = lax.psum(
        (jnp.sum(residual * residual), jnp.sum(direction * normal_image)), ("tile", "rank")
    )
    norm_now = norm_now + tiny_value
    step_size = norm_now / (curvature + tiny_value)
    new_step = step_now + step_size * direction
    new_residual = residual - step_size * normal_image
    norm_next = lax.psum(jnp.sum(new_residual * new_residual), ("tile", "rank"))
    new_direction = new_residual + norm_next / norm_now * direction
    return (new_step, new_residual, new_direction)


def split_bf16(x, parts):
    out = []
    for _ in range(parts):
        head = x.astype(jnp.bfloat16)
        out.append(head)
        x = x - head.astype(jnp.float32)
    return out


def dot_nt(a, b):
    return lax.dot_general(a, b, (((1,), (1,)), ((), ())), preferred_element_type=jnp.float32)


def dot_nn(a, b):
    return jnp.dot(a, b, preferred_element_type=jnp.float32)


def iota(shape, dim):
    return lax.broadcasted_iota(jnp.int32, shape, dim)


def cg_kernel(
    dims,
    residual_hbm,
    direction_hbm,
    perm_hbm,
    col_hbm,
    row_hbm,
    coupling_hbm,
    blocks_hbm,
    leaf_hbm,
    target_hbm,
    live_smem,
    weight_hbm,
    image_out,
    alpha_out,
    beta_out,
    residual_ref,
    direction_ref,
    perm_ref,
    leaf_ref,
    target_ref,
    weight_ref,
    col_ref,
    row_ref,
    coupling_ref,
    blocks_ref,
    onehot_ref,
    slots_ref,
    weight_s,
    far_s,
    weighted_f,
    a_send,
    a_recv,
    vec_f,
    res_f,
    b_send,
    b_recv,
    c_send,
    c_recv,
    d_send,
    d_recv,
    e_send,
    e_recv,
    far_back_s,
    image_s,
    f_recv,
    g_send,
    g_recv,
    values_s,
    load_sem,
    a_ss,
    a_rs,
    b_ss,
    b_rs,
    c_ss,
    c_rs,
    d_ss,
    d_rs,
    e_ss,
    e_rs,
    f_ss,
    f_rs,
    g_ss,
    g_rs,
):
    T, RK, NBS, KC, WR = dims
    bf16, f32 = jnp.bfloat16, jnp.float32
    rows = direction_hbm.shape[0]
    pr = rows // T
    G = weight_hbm.shape[1] // 128
    KG = KC * G
    gt = G * RK
    NBP = values_s.shape[0]
    KI = KC * LD
    t = lax.axis_index("tile")
    r = lax.axis_index("rank")
    me = t * RK + r

    def remote(src, dst, ss, rs, tile, rank):
        return pltpu.make_async_remote_copy(
            src_ref=src,
            dst_ref=dst,
            send_sem=ss,
            recv_sem=rs,
            device_id=(tile, rank),
            device_id_type=pl.DeviceIdType.MESH,
        )

    operands = [
        (direction_hbm, direction_ref),
        (perm_hbm, perm_ref),
        (residual_hbm, residual_ref),
        (leaf_hbm, leaf_ref),
        (target_hbm, target_ref),
        (weight_hbm, weight_ref),
        (col_hbm, col_ref),
        (blocks_hbm, blocks_ref),
        (coupling_hbm, coupling_ref),
        (row_hbm, row_ref),
    ]
    loads = [
        pltpu.make_async_copy(source, held, load_sem.at[i])
        for i, (source, held) in enumerate(operands)
    ]
    for load in loads:
        load.start()

    b_recv[...] = jnp.zeros_like(b_recv)
    e_recv[...] = jnp.zeros_like(e_recv)
    c_recv[...] = jnp.zeros_like(c_recv)
    d_recv[...] = jnp.zeros_like(d_recv)

    barrier = pltpu.get_barrier_semaphore()
    for dt in range(T):
        for dr in range(RK):
            if dt or dr:
                pl.semaphore_signal(
                    barrier,
                    inc=1,
                    device_id=(lax.rem(t + dt, T), lax.rem(r + dr, RK)),
                    device_id_type=pl.DeviceIdType.MESH,
                )

    for load in loads[:3]:
        load.wait()
    pieces = jnp.concatenate(
        split_bf16(direction_ref[...], 3) + split_bf16(residual_ref[...], 3), axis=0
    )
    for q in range(rows):
        perm = perm_ref[q : q + 1, :]
        low = lax.bitwise_and(perm, 127)
        high = lax.shift_right_logical(perm, 7)
        onehot = (iota((128, 128), 0) == low).astype(f32).astype(bf16)
        onehot_ref[q] = onehot
        looked = dot_nn(pieces, onehot)
        mask = iota((rows, 128), 0) == high
        d_rows = (looked[0:rows] + looked[rows : 2 * rows]) + looked[2 * rows : 3 * rows]
        r_rows = (looked[3 * rows : 4 * rows] + looked[4 * rows : 5 * rows]) + looked[5 * rows :]
        c, k = q // pr, q % pr
        a_send[c, k : k + 1, :] = jnp.sum(jnp.where(mask, d_rows, 0.0), axis=0, keepdims=True)
        a_send[c, pr + k : pr + k + 1, :] = jnp.sum(
            jnp.where(mask, r_rows, 0.0), axis=0, keepdims=True
        )

    pl.semaphore_wait(barrier, T * RK - 1)

    a_recv[t] = a_send[t]
    for off in range(1, T):
        c = lax.rem(t + off, T)
        remote(a_send.at[c], a_recv.at[t], a_ss.at[c], a_rs.at[t], c, r).start()

    for load in loads[3:8]:
        load.wait()
    slots_ref[...] = jnp.zeros_like(slots_ref)
    slots_ref[0:1, 0:NBS] = target_ref[...]
    slots_ref[1:2, 0:NBS] = leaf_ref[...]
    diagonal = iota((NBP, 128), 0) == iota((NBP, 128), 1)
    target_row = slots_ref[0:1, :]
    leaf_row = slots_ref[1:2, :]
    target_col = jnp.sum(jnp.where(diagonal, target_row, 0), axis=1, keepdims=True)
    leaf_col = jnp.sum(jnp.where(diagonal, leaf_row, 0), axis=1, keepdims=True)
    live = iota((1, 128), 1) < live_smem[0]
    spread_hot = (
        ((iota((3 * gt, 128), 0) == lax.shift_right_logical(target_row, 1)) & live)
        .astype(f32)
        .astype(bf16)[:, :NBP]
    )
    pick_hot = (iota((NBP, 3 * gt), 1) == lax.shift_right_logical(target_col, 1)).astype(f32).astype(bf16)
    leaf_hot = (iota((NBP, rows), 1) == leaf_col).astype(f32).astype(bf16)
    leaf_spread = ((iota((rows, 128), 0) == leaf_row) & live).astype(f32).astype(bf16)[:, :NBP]
    odd = lax.bitwise_and(target_col, 1) == 1
    upper = iota((NBP, 128), 1) >= LD
    for k in range(KC):
        for g in range(G):
            weight_s[k * G + g : k * G + g + 1, :] = weight_ref[k : k + 1, g * 128 : (g + 1) * 128]
    values_s[...] = jnp.zeros_like(values_s)

    for off in range(1, T):
        s = lax.rem(t + off, T)
        remote(a_send.at[s], a_recv.at[s], a_ss.at[s], a_rs.at[s], s, r).wait_recv()
    for s in range(T):
        vec_f[s * pr : (s + 1) * pr, :] = a_recv[s, 0:pr, :]
        res_f[s * pr : (s + 1) * pr, :] = a_recv[s, pr : 2 * pr, :]

    vec_row = jnp.concatenate([vec_f[q : q + 1, :] for q in range(rows)], axis=1).astype(bf16)
    b_send[:, 0:WR] = dot_nt(vec_row, col_ref[...])

    def far(c):
        return jnp.abs(c - t) > 1

    for off in range(1, T):
        c = lax.rem(t + off, T)

        @pl.when(far(c))
        def _():
            for k in range(RK):
                remote(
                    b_send, b_recv.at[me], b_ss.at[c * RK + k], b_rs.at[me], c, k
                ).start()

    picked = dot_nn(leaf_hot, vec_f[...].astype(bf16)).astype(bf16)
    for b in range(NBS):
        values_s[b : b + 1, :] = dot_nt(
            picked[b : b + 1, :], blocks_ref[b * KI : (b + 1) * KI, :]
        )
    for k in range(KC):
        part = values_s[:, (k // 2) * 128 : (k // 2 + 1) * 128]
        rolled = pltpu.roll(part, LD, 1)
        moved = jnp.where(odd, rolled, part) if k % 2 == 0 else jnp.where(odd, part, rolled)
        moved = jnp.where(upper == odd, moved, 0.0)
        head, tail = split_bf16(moved, 2)
        summed = dot_nn(spread_hot, head) + dot_nn(spread_hot, tail)
        for o in range(3):
            for k2 in range(RK):
                start = o * gt + k2 * G
                c_send[o, k2, k * G : (k + 1) * G, :] = summed[start : start + G, :]
    for o in range(3):
        for k2 in range(RK):
            c_out = c_send[o, k2].astype(bf16)
            c_bf = c_out
            d_send[1 + o * RK + k2] = c_bf

    def inside(c):
        return (c >= 0) & (c < T)

    def near_copies(source, landing, ss, rs, mirrored, act):
        for o in (0, 2, 1):
            there = t + (1 - o if mirrored else o - 1)

            @pl.when(inside(there))
            def _():
                for dr in range(RK):
                    if o == 1 and dr == 0:
                        continue
                    k2 = lax.rem(r + dr, RK)
                    act(
                        remote(
                            source(o, k2), landing.at[o, r], ss.at[o, k2], rs.at[o, r], there, k2
                        )
                    )

    def near_waits(landing, ss, rs, mirrored):
        for o in (1, 0, 2):
            there = t + (o - 1 if mirrored else 1 - o)

            @pl.when(inside(there))
            def _():
                for dr in range(RK):
                    if o == 1 and dr == 0:
                        continue
                    k2 = lax.rem(r + dr, RK)
                    remote(
                        landing.at[o, k2], landing.at[o, k2], ss.at[o, k2], rs.at[o, k2], t, k2
                    ).wait_recv()

    def c_source(o, k2):
        return d_send.at[1 + o * RK + k2]

    def d_source(o, k2):
        return d_send.at[0]

    near_copies(c_source, c_recv, c_ss, c_rs, False, lambda copy: copy.start())

    loads[8].wait()
    loads[9].wait()
    for off in range(1, T):
        c = lax.rem(t + off, T)

        @pl.when(far(c))
        def _():
            for k in range(RK):
                slot = c * RK + k
                remote(b_send, b_recv.at[slot], b_ss.at[slot], b_rs.at[slot], c, k).wait_recv()

    far_coef = jnp.zeros((1, WR), f32)
    for c in range(T):
        coef = b_recv[c * RK]
        for k in range(1, RK):
            coef = coef + b_recv[c * RK + k]
        far_coef = far_coef + dot_nt(coef[:, 0:WR].astype(bf16), coupling_ref[c])
    far_bf = far_coef.astype(bf16)
    for k in range(KC):
        far_row = dot_nn(far_bf, row_ref[k])
        for g in range(G):
            far_s[k * G + g : k * G + g + 1, :] = far_row[:, g * 128 : (g + 1) * 128]

    near_waits(c_recv, c_ss, c_rs, False)
    own = jnp.zeros((KG, 128), f32)
    for k2 in range(RK):
        own = own + jnp.where(r == k2, c_send[1, k2], 0.0)
    near = own
    for o in range(3):
        for k2 in range(RK):
            near = near + c_recv[o, k2].astype(f32)
    weighted = (weight_s[...] * (far_s[...] + near)).astype(bf16)
    d_send[0] = weighted
    weighted_f[...] = weighted.astype(f32)
    d_recv[1, r] = weighted

    back_part = jnp.zeros((1, WR), f32)
    for k in range(KC):
        weighted_row = jnp.concatenate(
            [weighted_f[k * G + g : k * G + g + 1, :] for g in range(G)], axis=1
        )
        back_part = back_part + dot_nt(weighted_row.astype(bf16), row_ref[k])
    back_two = jnp.concatenate(split_bf16(back_part, 2), axis=0)
    for c in range(T):
        two = dot_nn(back_two, coupling_ref[c])
        e_send[c, :, 0:WR] = two[0:1, :] + two[1:2, :]
    for off in range(1, T):
        c = lax.rem(t + off, T)

        @pl.when(far(c))
        def _():
            for k in range(RK):
                remote(
                    e_send.at[c], e_recv.at[me], e_ss.at[c * RK + k], e_rs.at[me], c, k
                ).start()

    near_copies(d_source, d_recv, d_ss, d_rs, True, lambda copy: copy.start())

    near_waits(d_recv, d_ss, d_rs, True)
    chosen = []
    for k in range(KC):
        window = jnp.concatenate(
            [
                d_recv[o, k2, :, :].astype(f32)[k * G : (k + 1) * G, :]
                for o in range(3)
                for k2 in range(RK)
            ],
            axis=0,
        ).astype(bf16)
        found = dot_nn(pick_hot, window)
        rolled = pltpu.roll(found, LD, 1)
        chosen.append(
            jnp.where(odd, rolled, found) if k % 2 == 0 else jnp.where(odd, found, rolled)
        )
    chosen_rows = jnp.concatenate(
        [jnp.where(upper, chosen[2 * m + 1], chosen[2 * m]) for m in range(KC // 2)], axis=1
    ).astype(bf16)
    for b in range(NBS):
        values_s[b : b + 1, 0:128] = dot_nn(
            chosen_rows[b : b + 1, :], blocks_ref[b * KI : (b + 1) * KI, :]
        )
    head, tail = split_bf16(values_s[:, 0:128], 2)
    near_back = dot_nn(leaf_spread, head) + dot_nn(leaf_spread, tail)

    for off in range(1, T):
        c = lax.rem(t + off, T)

        @pl.when(far(c))
        def _():
            for k in range(RK):
                slot = c * RK + k
                remote(e_send.at[c], e_recv.at[slot], e_ss.at[slot], e_rs.at[slot], c, k).wait_recv()

    cluster_back = jnp.zeros((1, 128), f32)
    for slot in range(T * RK):
        cluster_back = cluster_back + e_recv[slot]
    far_back = dot_nn(cluster_back[:, 0:WR].astype(bf16), col_ref[...])
    for q in range(rows):
        far_back_s[q : q + 1, :] = far_back[:, q * 128 : (q + 1) * 128]
    image = far_back_s[...] + near_back
    for s in range(T):
        image_s[s] = image[s * pr : (s + 1) * pr, :]
    for off in range(1, T):
        s = lax.rem(t + off, T)
        remote(image_s.at[s], f_recv.at[t], f_ss.at[s], f_rs.at[t], s, r).start()
    f_recv[t] = image_s[t]

    vec = vec_f[...]
    res = res_f[...]
    normal = image + damping_weight * vec

    def total(x):
        return jnp.sum(jnp.sum(x, axis=0, keepdims=True), axis=1, keepdims=True)

    lane = iota((1, 128), 1)
    sums = jnp.where(lane == 0, total(vec * normal), 0.0)
    sums = jnp.where(lane == 1, total(res * normal), sums)
    sums = jnp.where(lane == 2, total(normal * normal), sums)
    sums = jnp.where(lane == 3, total(res * res), sums)
    g_send[...] = sums
    g_recv[me] = sums
    others = [(dt, dr) for dt in range(T) for dr in range(RK) if dt or dr]
    for dt, dr in others:
        c, k = lax.rem(t + dt, T), lax.rem(r + dr, RK)
        remote(g_send, g_recv.at[me], g_ss.at[c * RK + k], g_rs.at[me], c, k).start()

    for off in range(1, T):
        s = lax.rem(t + off, T)
        remote(image_s.at[s], f_recv.at[s], f_ss.at[s], f_rs.at[s], s, r).wait_recv()
    back = jnp.zeros((3 * rows, 128), f32)
    for q in range(rows):
        perm = perm_ref[q : q + 1, :]
        high = lax.shift_right_logical(perm, 7)
        mask = iota((rows, 128), 0) == high
        entry = f_recv[q // pr, q % pr : q % pr + 1, :]
        parts = split_bf16(jnp.where(mask, entry, 0.0), 3)
        back = back + dot_nt(jnp.concatenate(parts, axis=0), onehot_ref[q])
    slab = (back[0:rows] + back[rows : 2 * rows]) + back[2 * rows :]
    image_out[...] = slab + damping_weight * direction_ref[...]

    for dt, dr in others:
        c, k = lax.rem(t + dt, T), lax.rem(r + dr, RK)
        slot = c * RK + k
        remote(g_send, g_recv.at[slot], g_ss.at[slot], g_rs.at[slot], c, k).wait_recv()
    sums = g_recv[0]
    for slot in range(1, T * RK):
        sums = sums + g_recv[slot]

    def pick(i):
        return jnp.sum(jnp.where(lane == i, sums, 0.0), axis=1, keepdims=True)

    norm_now = pick(3) + tiny_value
    alpha = norm_now / (pick(0) + tiny_value)
    norm_next = pick(3) - 2.0 * alpha * pick(1) + alpha * alpha * pick(2)
    beta = jnp.maximum(norm_next, 0.0) / norm_now
    alpha_out[...] = jnp.broadcast_to(alpha, alpha_out.shape)
    beta_out[...] = jnp.broadcast_to(beta, beta_out.shape)

    for off in range(1, T):
        c = lax.rem(t + off, T)
        remote(a_send.at[c], a_recv.at[t], a_ss.at[c], a_rs.at[t], c, r).wait_send()
        remote(image_s.at[c], f_recv.at[t], f_ss.at[c], f_rs.at[t], c, r).wait_send()

        @pl.when(far(c))
        def _():
            for k in range(RK):
                remote(b_send, b_recv.at[me], b_ss.at[c * RK + k], b_rs.at[me], c, k).wait_send()
                remote(
                    e_send.at[c], e_recv.at[me], e_ss.at[c * RK + k], e_rs.at[me], c, k
                ).wait_send()

    near_copies(c_source, c_recv, c_ss, c_rs, False, lambda copy: copy.wait_send())
    near_copies(d_source, d_recv, d_ss, d_rs, True, lambda copy: copy.wait_send())
    for dt, dr in others:
        c, k = lax.rem(t + dt, T), lax.rem(r + dr, RK)
        remote(g_send, g_recv.at[me], g_ss.at[c * RK + k], g_rs.at[me], c, k).wait_send()


def fused(
    step_now,
    residual,
    direction,
    slab_perm,
    col_basis,
    row_basis,
    coupling,
    near_blocks,
    near_leaf,
    near_target,
    near_live,
    data_weight,
):
    T, RK = lax.axis_size("tile"), lax.axis_size("rank")
    N = T * RK
    rows = direction.shape[0] // 128
    pr = rows // T
    NBS, KC = near_blocks.shape[0], near_blocks.shape[1]
    WR = col_basis.shape[0]
    G = data_weight.shape[1] // 128
    KG = KC * G
    NBP = -(-NBS // 16) * 16
    f32, bf16 = jnp.float32, jnp.bfloat16
    res2 = residual.reshape(rows, 128)
    dir2 = direction.reshape(rows, 128)
    vmem = pl.BlockSpec(memory_space=pltpu.VMEM)
    hbm = pl.BlockSpec(memory_space=pltpu.HBM)
    row3 = row_basis.transpose(1, 0, 2)
    blocks2 = near_blocks.reshape(-1, LEAF)
    sem = pltpu.SemaphoreType.DMA
    out = jax.ShapeDtypeStruct((rows, 128), f32)
    image, alpha, beta = pl.pallas_call(
        functools.partial(cg_kernel, (T, RK, NBS, KC, WR)),
        out_shape=(out, out, out),
        in_specs=[hbm] * 9 + [pl.BlockSpec(memory_space=pltpu.SMEM), hbm],
        out_specs=(vmem, vmem, vmem),
        scratch_shapes=[
            pltpu.VMEM((rows, 128), f32),
            pltpu.VMEM((rows, 128), f32),
            pltpu.VMEM((rows, 128), jnp.int32),
            pltpu.VMEM((1, NBS), jnp.int32),
            pltpu.VMEM((1, NBS), jnp.int32),
            pltpu.VMEM(data_weight.shape, f32),
            pltpu.VMEM(col_basis.shape, bf16),
            pltpu.VMEM(row3.shape, bf16),
            pltpu.VMEM(coupling.shape[1:], bf16),
            pltpu.VMEM(blocks2.shape, bf16),
            pltpu.VMEM((rows, 128, 128), bf16),
            pltpu.VMEM((8, 128), jnp.int32),
            pltpu.VMEM((KG, 128), f32),
            pltpu.VMEM((KG, 128), f32),
            pltpu.VMEM((KG, 128), f32),
            pltpu.VMEM((T, 2 * pr, 128), f32),
            pltpu.VMEM((T, 2 * pr, 128), f32),
            pltpu.VMEM((rows, 128), f32),
            pltpu.VMEM((rows, 128), f32),
            pltpu.VMEM((1, 128), f32),
            pltpu.VMEM((N, 1, 128), f32),
            pltpu.VMEM((3, RK, KG, 128), f32),
            pltpu.VMEM((3, RK, KG, 128), bf16),
            pltpu.VMEM((1 + 3 * RK, KG, 128), bf16),
            pltpu.VMEM((3, RK, KG, 128), bf16),
            pltpu.VMEM((T, 1, 128), f32),
            pltpu.VMEM((N, 1, 128), f32),
            pltpu.VMEM((rows, 128), f32),
            pltpu.VMEM((T, pr, 128), f32),
            pltpu.VMEM((T, pr, 128), f32),
            pltpu.VMEM((1, 128), f32),
            pltpu.VMEM((N, 1, 128), f32),
            pltpu.VMEM((NBP, KC * LD), f32),
            sem((10,)),
            sem((T,)),
            sem((T,)),
            sem((N,)),
            sem((N,)),
            sem((3, RK)),
            sem((3, RK)),
            sem((3, RK)),
            sem((3, RK)),
            sem((N,)),
            sem((N,)),
            sem((T,)),
            sem((T,)),
            sem((N,)),
            sem((N,)),
        ],
        compiler_params=pltpu.CompilerParams(
            collective_id=0, has_side_effects=True, vmem_limit_bytes=64 * 1024 * 1024
        ),
    )(
        res2,
        dir2,
        slab_perm.reshape(rows, 128),
        col_basis,
        row3,
        coupling[0],
        blocks2,
        near_leaf.reshape(1, NBS),
        near_target.reshape(1, NBS),
        near_live,
        data_weight,
    )
    new_step = step_now.reshape(rows, 128) + alpha * dir2
    new_residual = res2 - alpha * image
    new_direction = new_residual + beta * dir2
    return tuple(x.reshape(-1) for x in (new_step, new_residual, new_direction))


def solution(mesh):
    def body(*args):
        piece = args[2].shape[0] // mesh.shape["tile"]
        return (per_device if piece % 128 else fused)(*args)

    return jax.shard_map(
        body,
        mesh=mesh,
        in_specs=(
            P(("tile", "rank")),
            P(("tile", "rank")),
            P(("tile", "rank")),
            P(("tile", "rank")),
            P(None, ("tile", "rank")),
            P(None, None, ("tile", "rank")),
            P("tile", None, None, None),
            P(("tile", "rank"), None, None, None),
            P(("tile", "rank")),
            P(("tile", "rank")),
            P(("tile", "rank")),
            P(None, ("tile", "rank")),
        ),
        out_specs=(P(("tile", "rank")), P(("tile", "rank")), P(("tile", "rank"))),
        check_vma=False,
    )
```
